32 devices in a mesh: gx: 8 (over y, x, core), gy: 4 (over z).
Axes of the slice: x: 2, y: 2, z: 4, core: 2. Of those that a mesh axis runs over, the one named last changes fastest.
Arguments:
- velocity: float32 [2, 3, 384, 512], P(None, None, 'gx', 'gy'), may hold values from -6 to 6
- stretch: float32 [512], replicated, may hold values from 0.7 to 1.4
- second_metric: float32 [512], replicated, may hold values from -1 to 1
Outputs:
- section_rhs: float32 [2, 3, 384, 512], P(None, None, 'gx', 'gy')
The draws below stay inside these ranges and needn't reach their ends.
All inputs are finite; a program needn't handle non-finite values.
Results may differ from the reference program's by a relative error of at most 0.000054.
Values sent between devices are 32-bit elements; how exact they have to be, the bound alone decides.
No kernel may reach another device: no remote copies, remote signals or barrier semaphores. Data moves between devices by JAX's collectives and lax.ppermute only.
A program may use at most 64 MiB of HBM per device.

```python
import math
import jax
import jax.numpy as jnp
from jax import lax

SZ = 2
NX = 384
NY = 512


def levels(rng, extent, pieces, low, high):
    loudness = 1.0
    for axis_at, blocks in pieces:
        steps = jax.random.uniform(jax.random.fold_in(jax.random.fold_in(rng, 6), axis_at), (blocks,), jnp.float32, low / len(pieces), high / len(pieces))
        loudness = loudness * jnp.repeat(jnp.exp(steps), extent[axis_at] // blocks).reshape((-1,) + (1,) * (len(extent) - 1 - axis_at))
    return loudness


def noise(rng, dims, deviation, limit, pieces=(), kind=jnp.bfloat16):
    drawn = jax.random.normal(rng, dims, jnp.float32) * deviation
    if len(pieces) > 0:
        drawn = levels(rng, dims, pieces, -0.22, 0.18) * drawn
    return jnp.clip(drawn, min=-limit, max=limit).astype(kind)


def setup_inputs(seed: int = 0) -> dict:
    streams_of = jax.random.split(jax.random.key(seed), 4)
    return {
        "velocity": noise(streams_of[0], (SZ, 3, NX, NY), 1.0, 6.0, ((2, 8), (3, 4)), jnp.float32),
        "stretch": jnp.clip(jnp.exp(jax.random.uniform(streams_of[1], (NY,), jnp.float32, math.log(0.7), math.log(1.4))), 0.7, 1.4),
        "second_metric": jnp.clip(jax.random.uniform(streams_of[2], (NY,), jnp.float32, -1.0, 1.0), -1.0, 1.0),
    }


VISCOSITY = 0.5

def x_stencils(padded, length):
    axis_pos = padded.ndim - 2
    centre = lax.slice_in_dim(padded, 2, 2 + length, axis=axis_pos)
    plus_one = lax.slice_in_dim(padded, 3, 3 + length, axis=axis_pos)
    minus_one = lax.slice_in_dim(padded, 1, 1 + length, axis=axis_pos)
    plus_two = lax.slice_in_dim(padded, 4, 4 + length, axis=axis_pos)
    minus_two = lax.slice_in_dim(padded, 0, length, axis=axis_pos)
    first_rhs = 7.0 / 9.0 * (plus_one - minus_one) + 1.0 / 36.0 * (plus_two - minus_two)
    second = 12.0 / 11.0 * (plus_one - 2.0 * centre + minus_one) + 3.0 / 44.0 * (plus_two - 2.0 * centre + minus_two)
    return (first_rhs, second)

def y_stencils(padded, local, row_ids, total_rows):
    length = local.shape[-1]
    centre = padded[..., 2:2 + length]
    plus_one = padded[..., 3:3 + length]
    minus_one = padded[..., 1:1 + length]
    plus_two = padded[..., 4:4 + length]
    minus_two = padded[..., 0:length]
    near_wall = (row_ids == 1) | (row_ids == total_rows - 2)
    start_edge = row_ids == 0
    end_edge = row_ids == total_rows - 1
    head_rows = local[..., 0:4]
    tail_rows = local[..., length - 4:length]
    first_start = (-3.0 * head_rows[..., 0:1] + 4.0 * head_rows[..., 1:2] - head_rows[..., 2:3]) / 2.0
    first_end = (3.0 * tail_rows[..., 3:4] - 4.0 * tail_rows[..., 2:3] + tail_rows[..., 1:2]) / 2.0
    second_start = 2.0 * head_rows[..., 0:1] - 5.0 * head_rows[..., 1:2] + 4.0 * head_rows[..., 2:3] - head_rows[..., 3:4]
    second_end = 2.0 * tail_rows[..., 3:4] - 5.0 * tail_rows[..., 2:3] + 4.0 * tail_rows[..., 1:2] - tail_rows[..., 0:1]
    inner_first = 7.0 / 9.0 * (plus_one - minus_one) + 1.0 / 36.0 * (plus_two - minus_two)
    inner_second = 12.0 / 11.0 * (plus_one - 2.0 * centre + minus_one) + 3.0 / 44.0 * (plus_two - 2.0 * centre + minus_two)
    first_rhs = jnp.where(near_wall, 0.75 * (plus_one - minus_one), inner_first)
    first_rhs = jnp.where(start_edge, first_start, jnp.where(end_edge, first_end, first_rhs))
    second = jnp.where(near_wall, 1.2 * (plus_one - 2.0 * centre + minus_one), inner_second)
    second = jnp.where(start_edge, second_start, jnp.where(end_edge, second_end, second))
    return (first_rhs, second)

def y_coefs(row_ids, total_rows):
    near_wall = (row_ids == 1) | (row_ids == total_rows - 2)
    edge_rows = (row_ids == 0) | (row_ids == total_rows - 1)
    band_one = jnp.where(edge_rows, 0.0, jnp.where(near_wall, 0.25, 1.0 / 3.0))
    band_two = jnp.where(edge_rows, 0.0, jnp.where(near_wall, 0.1, 2.0 / 11.0))
    return (band_one, band_two)

def cyclic_solve(right_side, coefficient):
    length = right_side.shape[-2]
    moved = jnp.moveaxis(right_side, -2, 0)
    moved_shape = moved.shape
    columns = moved.reshape(length, -1)
    indices = jnp.arange(length)
    side_band = jnp.full((length,), coefficient, dtype=right_side.dtype)
    lower_band = jnp.where(indices == 0, 0.0, side_band).astype(right_side.dtype)
    upper_band = jnp.where(indices == length - 1, 0.0, side_band).astype(right_side.dtype)
    centre_band = jnp.where(indices == 0, 2.0, jnp.where(indices == length - 1, 1.0 + coefficient * coefficient, 1.0)).astype(right_side.dtype)
    column = jnp.where(indices == 0, -1.0, jnp.where(indices == length - 1, coefficient, 0.0)).astype(right_side.dtype)
    stacked = jnp.concatenate([columns, column[:, None]], axis=1)
    solved = lax.linalg.tridiagonal_solve(lower_band, centre_band, upper_band, stacked)
    base_part = solved[:, :-1]
    spread = solved[:, -1]
    factor = (base_part[0] - coefficient * base_part[-1]) / (1.0 + spread[0] - coefficient * spread[-1])
    result = base_part - spread[:, None] * factor[None, :]
    return jnp.moveaxis(result.reshape(moved_shape), 0, -2)

def band_solve(right_side, band_coef):
    length = right_side.shape[-1]
    moved = jnp.moveaxis(right_side, -1, 0)
    moved_shape = moved.shape
    columns = moved.reshape(length, -1)
    band_coef = band_coef.astype(right_side.dtype)
    diagonal = jnp.ones((length,), right_side.dtype)
    solved = lax.linalg.tridiagonal_solve(band_coef, diagonal, band_coef, columns)
    return jnp.moveaxis(solved.reshape(moved_shape), 0, -1)

def plane_terms(velocity_plane, stretch, second_metric):
    padded_x = jnp.concatenate([velocity_plane[:, -2:, :], velocity_plane, velocity_plane[:, :2, :]], axis=1)
    first_x, second_x = x_stencils(padded_x, NX)
    grad_x = cyclic_solve(first_x, 1.0 / 3.0)
    curv_x = cyclic_solve(second_x, 2.0 / 11.0)
    padded_y = jnp.pad(velocity_plane, ((0, 0), (0, 0), (2, 2)))
    row_ids = jnp.arange(NY)
    first_y, second_y = y_stencils(padded_y, velocity_plane, row_ids, NY)
    band_one, band_two = y_coefs(row_ids, NY)
    eta_one = band_solve(first_y, band_one)
    eta_two = band_solve(second_y, band_two)
    grad_y = eta_one / stretch
    curv_y = eta_two / (stretch * stretch) - second_metric * eta_one / (stretch * stretch * stretch)
    return -(velocity_plane[0:1] * grad_x + velocity_plane[1:2] * grad_y) + VISCOSITY * (curv_x + curv_y)

def reference(velocity, stretch, second_metric):
    return lax.map(lambda plane_vel: plane_terms(plane_vel, stretch, second_metric), velocity)
```

```python
import functools

import jax
import jax.numpy as jnp
import numpy as np
from jax import lax
from jax.experimental import pallas as pl
from jax.experimental.pallas import tpu as pltpu
from jax.sharding import PartitionSpec as P

VISCOSITY = 0.5
COEFS = (1.0 / 3.0, 2.0 / 11.0)
WALL_COEFS = (1.0 / 4.0, 1.0 / 10.0)
HIGHEST = lax.Precision.HIGHEST


def decay(coef):
    root = (-1.0 + np.sqrt(1.0 - 4.0 * coef * coef)) / (2.0 * coef)
    return root, 1.0 / (1.0 + 2.0 * coef * root)


def toeplitz(coef, length):
    root, gain = decay(coef)
    at = np.arange(length)
    return gain * root ** np.abs(at[:, None] - at[None, :])


def wall_columns(coef, wall_coef, length):
    root, gain = decay(coef)
    size = length + 64
    band = np.full(size, coef)
    band[0], band[1] = 0.0, wall_coef
    matrix = np.eye(size) + np.diag(band[:-1], 1) + np.diag(band[1:], -1)
    inverse = np.linalg.solve(matrix, np.eye(size)[:, :3])
    at = np.arange(size)
    spread = (inverse[:, 2] - gain * root ** np.abs(at - 2.0)) / root**2
    return np.stack([inverse[:, 0], inverse[:, 1], spread], axis=1)[:length]


def inner_columns(coef, length):
    root, gain = decay(coef)
    at = np.arange(length)
    return gain * np.stack([root**at, root ** np.abs(at - 1.0), root ** (at + 1.0)], axis=1)


def edge_table(length, low_wall, high_wall):
    table = np.zeros((16, 2 * length))
    for system in range(2):
        sign = -1.0 if system == 0 else 1.0
        inner = inner_columns(COEFS[system], length)
        wall = wall_columns(COEFS[system], WALL_COEFS[system], length)
        low = wall if low_wall else inner
        high = wall if high_wall else inner
        part = slice(system * length, (system + 1) * length)
        table[6 * system : 6 * system + 3, part] = low.T
        table[6 * system + 3 : 6 * system + 6, part] = high[::-1].T
    return table.astype(np.float32)


def stencils(minus_two, minus_one, centre, plus_one, plus_two):
    first = 7.0 / 9.0 * (plus_one - minus_one) + 1.0 / 36.0 * (plus_two - minus_two)
    second = 12.0 / 11.0 * (plus_one - 2.0 * centre + minus_one) + 3.0 / 44.0 * (
        plus_two - 2.0 * centre + minus_two
    )
    return first, second


def row_stencils(field):
    rows = field.shape[-2]
    cut = lambda at: field[..., at : at + rows - 4, :]
    return stencils(cut(0), cut(1), cut(2), cut(3), cut(4))


def lane_stencils(field):
    lanes = field.shape[-1]
    axis = field.ndim - 1
    turn = lambda steps: pltpu.roll(field, steps % lanes, axis)
    return stencils(turn(2), turn(1), field, turn(-1), turn(-2))


def send_kernel(field, x_weights, y_weights, xe_out, xo_out, ye_out, yo_out):
    slabs, rows, lanes = field.shape
    x_even = lax.rem(lax.axis_index("gx"), 2) == 0
    y_even = lax.rem(lax.axis_index("gy"), 2) == 0
    value = field[...]
    first, second = row_stencils(value)
    zeros = jnp.zeros((2, lanes), jnp.float32)
    for s in range(slabs):
        sums = [
            jnp.sum(x_weights[k] * part[s], axis=0, keepdims=True)
            for k, part in enumerate((first, second, first, second))
        ]
        low = jnp.concatenate([value[s, 0:4], sums[0], sums[1], zeros], axis=0)
        high = jnp.concatenate([value[s, rows - 4 : rows], sums[2], sums[3], zeros], axis=0)
        place = pl.ds(s * lanes, lanes)
        xe_out[:, place] = jnp.where(x_even, high, low)
        xo_out[:, place] = jnp.where(x_even, low, high)
    flat = value.reshape(slabs * rows, lanes)
    first, second = lane_stencils(flat)
    contract = (((1,), (1,)), ((), ()))
    packed = sum(
        lax.dot_general(
            y_weights[k], part, contract, precision=HIGHEST, preferred_element_type=jnp.float32
        )
        for k, part in enumerate((flat, first, second))
    )
    ye_out[...] = jnp.where(y_even, packed[8:], packed[:8])
    yo_out[...] = jnp.where(y_even, packed[:8], packed[8:])


def metric_rows(stretch, metric):
    position = lax.axis_index("gy")
    inv = 1.0 / stretch[pl.ds(position, 1), :]
    curve = metric[pl.ds(position, 1), :]
    return inv, VISCOSITY * curve * inv * inv * inv, VISCOSITY * inv * inv


def combine(velocity_u, velocity_v, grad_x, curv_x, eta_one, eta_two, rows):
    inv, slope, bend = rows
    return (
        VISCOSITY * curv_x + bend * eta_two - velocity_u * grad_x - (velocity_v * inv + slope) * eta_one
    )


def bulk_kernel(field, stretch, metric, x_matrix, y_matrix, out):
    slabs, rows, lanes = field.shape
    value = field[...]
    flat = value.reshape(slabs * rows, lanes)
    lane = lax.broadcasted_iota(jnp.int32, flat.shape, 1)
    inner = (lane >= 2) & (lane < lanes - 2)
    eta = [
        jnp.dot(
            jnp.where(inner, part, 0.0),
            y_matrix[k],
            precision=HIGHEST,
            preferred_element_type=jnp.float32,
        ).reshape(slabs, rows, lanes)
        for k, part in enumerate(lane_stencils(flat))
    ]
    pad = jnp.zeros((2, lanes), jnp.float32)
    solved = [
        [
            jnp.dot(
                x_matrix[k],
                jnp.concatenate([pad, part[s], pad], axis=0),
                precision=HIGHEST,
                preferred_element_type=jnp.float32,
            )
            for s in range(slabs)
        ]
        for k, part in enumerate(row_stencils(value))
    ]
    metrics = metric_rows(stretch, metric)
    for s in range(slabs):
        plane = s // 3 * 3
        out[s] = combine(
            value[plane], value[plane + 1], solved[0][s], solved[1][s], eta[0][s], eta[1][s], metrics
        )


def edge_rows(own, other, far_sums, roots, sign):
    a1, a2, a3, a4 = own
    b1, b2, b3, b4 = other
    f0, s0 = stencils(b2, b1, a1, a2, a3)
    f1, s1 = stencils(b1, a1, a2, a3, a4)
    g1, t1 = stencils(b3, b2, b1, a1, a2)
    g2, t2 = stencils(b4, b3, b2, b1, a1)
    first_sum = sign * (g1 + roots[0] * g2) + far_sums[0]
    second_sum = t1 + roots[1] * t2 + far_sums[1]
    return (sign * f0, sign * f1, first_sum), (s0, s1, second_sum)


def wall_rows(own, own_sums, sign):
    a1, a2, a3, a4 = own
    first = (
        sign * 0.5 * (4.0 * a2 - 3.0 * a1 - a3),
        sign * 0.75 * (a3 - a1),
        own_sums[0],
    )
    second = (2.0 * a1 - 5.0 * a2 + 4.0 * a3 - a4, 1.2 * (a3 - 2.0 * a2 + a1), own_sums[1])
    return first, second


def layers(packed, ascending):
    rows = [packed[k : k + 1] for k in range(4)]
    return rows if ascending else rows[::-1]


def far(packed):
    return packed[4:5], packed[5:6]


def edge_matrix(own_low, own_high, other_low, other_high, low_wall=None, high_wall=None):
    roots = [decay(coef)[0] for coef in COEFS]
    low = edge_rows(layers(own_low, True), layers(other_low, False), far(other_low), roots, 1.0)
    high = edge_rows(layers(own_high, False), layers(other_high, True), far(other_high), roots, -1.0)
    if low_wall is not None:
        at_low = wall_rows(layers(own_low, True), far(own_low), 1.0)
        at_high = wall_rows(layers(own_high, False), far(own_high), -1.0)
        low = jax.tree.map(lambda wall, inner: jnp.where(low_wall, wall, inner), at_low, low)
        high = jax.tree.map(lambda wall, inner: jnp.where(high_wall, wall, inner), at_high, high)
    rows = [*low[0], *high[0], *low[1], *high[1]]
    rows.append(jnp.zeros((4, rows[0].shape[1]), jnp.float32))
    return jnp.concatenate(rows, axis=0)


def final_kernel(
    field, stretch, metric, x_table, y_table, bulk, xe_own, xo_own, ye_own, yo_own, xe, xo, ye, yo, out
):
    slabs, rows, lanes = field.shape
    y_at, y_count = lax.axis_index("gy"), lax.axis_size("gy")
    x_even = lax.rem(lax.axis_index("gx"), 2) == 0
    y_even = lax.rem(y_at, 2) == 0
    pick = lambda flag, one, two: jnp.where(flag, one[...], two[...])
    x_edges = edge_matrix(
        pick(x_even, xo_own, xe_own),
        pick(x_even, xe_own, xo_own),
        pick(x_even, xo, xe),
        pick(x_even, xe, xo),
    )
    y_edges = edge_matrix(
        pick(y_even, yo_own, ye_own),
        pick(y_even, ye_own, yo_own),
        pick(y_even, yo, ye),
        pick(y_even, ye, yo),
        y_at == 0,
        y_at == y_count - 1,
    )
    variant = jnp.where(y_at == 0, 0, jnp.where(y_at == y_count - 1, 2, 1))
    grad = lax.dot_general(
        x_table[...],
        x_edges,
        (((0,), (0,)), ((), ())),
        precision=HIGHEST,
        preferred_element_type=jnp.float32,
    )
    eta = lax.dot_general(
        y_edges,
        y_table[variant],
        (((0,), (0,)), ((), ())),
        precision=HIGHEST,
        preferred_element_type=jnp.float32,
    ).reshape(slabs, rows, 2 * lanes)
    metrics = metric_rows(stretch, metric)
    for s in range(slabs):
        plane = s // 3 * 3
        place = slice(s * lanes, (s + 1) * lanes)
        out[s] = bulk[s] + combine(
            field[plane],
            field[plane + 1],
            grad[:rows, place],
            grad[rows:, place],
            eta[s, :, :lanes],
            eta[s, :, lanes:],
            metrics,
        )


def exchange_pairs(x_count, y_count):
    at = lambda x, y: x * y_count + y
    x_even = lambda x: x ^ 1
    x_odd = lambda x: (x + 1) % x_count if x % 2 else (x - 1) % x_count
    cells = [(x, y) for x in range(x_count) for y in range(y_count)]
    xe = [(at(x, y), at(x_even(x), y)) for x, y in cells]
    xo = [(at(x, y), at(x_odd(x), y)) for x, y in cells]
    ye = [(at(x, y), at(x, y ^ 1)) for x, y in cells]
    yo = [
        (at(x, y), at(x_even(x), y) if y in (0, y_count - 1) else at(x, y + 1 if y % 2 else y - 1))
        for x, y in cells
    ]
    return xe, xo, ye, yo


def call(kernel, outs, name, flops, bytes_accessed):
    vmem = pl.BlockSpec(memory_space=pltpu.VMEM)
    many = isinstance(outs, list)
    return lambda *args: pl.pallas_call(
        kernel,
        out_shape=outs,
        in_specs=[vmem] * len(args),
        out_specs=[vmem] * len(outs) if many else vmem,
        cost_estimate=pl.CostEstimate(flops=flops, bytes_accessed=bytes_accessed, transcendentals=0),
        name=name,
    )(*args)


def shards(velocity, stretch, second_metric):
    planes, comps, rows, lanes = velocity.shape
    slabs = planes * comps
    x_count, y_count = lax.axis_size("gx"), lax.axis_size("gy")
    field = velocity.reshape(slabs, rows, lanes)
    stretch = stretch.reshape(y_count, lanes)
    metric = second_metric.reshape(y_count, lanes)
    roots = [decay(coef)[0] for coef in COEFS]

    at = np.arange(2, rows - 2)[:, None]
    x_weights = np.stack(
        [np.broadcast_to(w, (rows - 4, lanes)) for w in (*(r**at for r in roots), *(r ** (rows - 1 - at) for r in roots))]
    ).astype(np.float32)
    at = np.arange(2, lanes - 2)
    y_weights = np.zeros((3, 16, lanes), np.float32)
    for k in range(4):
        y_weights[0, k, k] = 1.0
        y_weights[0, 8 + k, lanes - 4 + k] = 1.0
    for k, r in enumerate(roots):
        y_weights[1 + k, 4 + k, 2:-2] = r**at
        y_weights[1 + k, 12 + k, 2:-2] = r ** (lanes - 1 - at)
    x_matrix = np.stack([toeplitz(coef, rows) for coef in COEFS]).astype(np.float32)
    y_matrix = np.stack([toeplitz(coef, lanes) for coef in COEFS]).astype(np.float32)
    x_table = edge_table(rows, False, False)
    y_table = np.stack(
        [edge_table(lanes, True, False), edge_table(lanes, False, False), edge_table(lanes, False, True)]
    )

    shape = lambda *dims: jax.ShapeDtypeStruct(dims, jnp.float32)
    x_shape, y_shape = shape(8, slabs * lanes), shape(8, slabs * rows)
    xe, xo, ye, yo = call(send_kernel, [x_shape, x_shape, y_shape, y_shape], "sends", 10**6, 10**6)(
        field, x_weights, y_weights
    )
    pairs = exchange_pairs(x_count, y_count)
    move = lambda value, way: lax.ppermute(value, ("gx", "gy"), way)
    xo_in = move(xo, pairs[1])
    ye_in = move(ye, pairs[2])
    xe_in = move(xe, pairs[0])
    yo_in = move(yo, pairs[3])
    bulk = call(bulk_kernel, shape(slabs, rows, lanes), "bulk", 10**8, 10**6)(
        field, stretch, metric, x_matrix, y_matrix
    )
    out = call(final_kernel, shape(slabs, rows, lanes), "final", 10**7, 10**6)(
        field, stretch, metric, x_table, y_table, bulk, xe, xo, ye, yo, xe_in, xo_in, ye_in, yo_in
    )
    return out.reshape(planes, comps, rows, lanes)


def solution(mesh):
    return jax.shard_map(
        shards,
        mesh=mesh,
        in_specs=(P(None, None, "gx", "gy"), P(), P()),
        out_specs=P(None, None, "gx", "gy"),
        check_vma=False,
    )
```

```python
import jax
import jax.numpy as jnp
import numpy as np
from jax import lax
from jax.experimental import pallas as pl
from jax.experimental.pallas import tpu as pltpu
from jax.sharding import PartitionSpec as P

VISCOSITY = 0.5
COEFS = (1.0 / 3.0, 2.0 / 11.0)
WALL_COEFS = (1.0 / 4.0, 1.0 / 10.0)
HIGHEST = lax.Precision.HIGHEST
TILE = 8


def decay(coef):
    root = (-1.0 + np.sqrt(1.0 - 4.0 * coef * coef)) / (2.0 * coef)
    return float(root), float(1.0 / (1.0 + 2.0 * coef * root))


ROOTS = tuple(decay(coef)[0] for coef in COEFS)


def inner_weights(system):
    root, gain = decay(COEFS[system])
    return (gain, gain / root, gain * root), (gain, gain * root, gain * root)


def wall_weights(system):
    root, gain = decay(COEFS[system])
    size = 96
    band = np.full(size, COEFS[system])
    band[0], band[1] = 0.0, WALL_COEFS[system]
    matrix = np.eye(size) + np.diag(band[:-1], 1) + np.diag(band[1:], -1)
    inverse = np.linalg.solve(matrix, np.eye(size)[:, :3])
    spread = (inverse[:2, 2] - gain * root ** np.abs(np.arange(2) - 2.0)) / root**2
    columns = np.stack([inverse[:2, 0], inverse[:2, 1], spread], axis=1)
    return tuple(map(float, columns[1] / root)), tuple(map(float, columns[0]))


def iota(shape, axis):
    return lax.broadcasted_iota(jnp.int32, shape, axis)


def powers(root, exponent):
    size = jnp.exp(exponent.astype(jnp.float32) * float(np.log(-root)))
    return jnp.where(lax.rem(exponent, 2) == 0, size, -size)


def stencils(minus_two, minus_one, centre, plus_one, plus_two):
    first = 7.0 / 9.0 * (plus_one - minus_one) + 1.0 / 36.0 * (plus_two - minus_two)
    second = 12.0 / 11.0 * (plus_one - 2.0 * centre + minus_one) + 3.0 / 44.0 * (
        plus_two - 2.0 * centre + minus_two
    )
    return first, second


def right_sides(lines):
    turn = lambda steps: pltpu.roll(lines, steps % lines.shape[0], 0)
    at = iota(lines.shape, 0)
    inner = (at >= 2) & (at < lines.shape[0] - 2)
    parts = stencils(turn(2), turn(1), lines, turn(-1), turn(-2))
    return [jnp.where(inner, part, 0.0) for part in parts]


def edge_sums(part, root):
    rows, lanes = part.shape
    tiles = [part[k : k + TILE] for k in range(0, rows, TILE)]
    step = float(root**TILE)
    low, high = tiles[-1], tiles[0]
    for tile in tiles[-2::-1]:
        low = low * step + tile
    for tile in tiles[1:]:
        high = high * step + tile
    at = iota((TILE, lanes), 0)
    low = low * powers(root, at)
    high = high * powers(root, TILE - 1 - at)
    return jnp.sum(low, axis=0, keepdims=True), jnp.sum(high, axis=0, keepdims=True)


def packed_edges(lines):
    rows, lanes = lines.shape
    sums = [edge_sums(part, root) for part, root in zip(right_sides(lines), ROOTS)]
    zeros = jnp.zeros((2, lanes), jnp.float32)
    low = jnp.concatenate([lines[0:4], sums[0][0], sums[1][0], zeros], axis=0)
    high = jnp.concatenate([lines[rows - 4 : rows], sums[0][1], sums[1][1], zeros], axis=0)
    return low, high


def send_kernel(field, ye_out, xo_out, yo_out, xe_out):
    slabs, rows, lanes = field.shape
    x_even = lax.rem(lax.axis_index("gx"), 2) == 0
    y_even = lax.rem(lax.axis_index("gy"), 2) == 0
    for s in range(slabs):
        low, high = packed_edges(field[s])
        place = pl.ds(s * lanes, lanes)
        xe_out[:, place] = jnp.where(x_even, high, low)
        xo_out[:, place] = jnp.where(x_even, low, high)
    low, high = packed_edges(jnp.transpose(field[...].reshape(slabs * rows, lanes)))
    place = pl.ds(0, slabs * rows)
    ye_out[:, place] = jnp.where(y_even, high, low)
    yo_out[:, place] = jnp.where(y_even, low, high)


def inverse_matrix(system, size):
    root, gain = decay(COEFS[system])
    return gain * powers(root, jnp.abs(iota((size, size), 0) - iota((size, size), 1)))


def solve(matrix, right_side):
    return jnp.dot(matrix, right_side, precision=HIGHEST, preferred_element_type=jnp.float32)


def bulk_kernel(field, stretch, metric, out, slope_turned, bend_turned):
    slabs, rows, lanes = field.shape
    position = pl.ds(lax.axis_index("gy"), 1)
    inv = 1.0 / stretch[position, :]
    curve = VISCOSITY * metric[position, :] * inv * inv * inv
    bend = jnp.transpose(jnp.broadcast_to(VISCOSITY * inv * inv, (lanes, lanes)))
    bend_turned[...] = bend
    slope = [-(field[plane * 3 + 1] * inv + curve) for plane in range(slabs // 3)]
    slope = jnp.transpose(jnp.concatenate([part for part in slope for _ in range(3)], axis=0))
    slope_turned[...] = slope
    first, second = right_sides(jnp.transpose(field[...].reshape(slabs * rows, lanes)))
    y_term = slope * solve(inverse_matrix(0, lanes), first)
    y_term += bend[:, :1] * solve(inverse_matrix(1, lanes), second)
    y_term = jnp.transpose(y_term)
    matrices = [inverse_matrix(system, rows) for system in range(2)]
    for s in range(slabs):
        first, second = right_sides(field[s])
        x_term = VISCOSITY * solve(matrices[1], second) - field[s // 3 * 3] * solve(matrices[0], first)
        out[s] = x_term + y_term[s * rows : (s + 1) * rows]


def edge_rows(own, other, sign):
    a1, a2, a3, a4 = layers(own, sign > 0)
    b1, b2, b3, b4 = layers(other, sign < 0)
    f0, s0 = stencils(b2, b1, a1, a2, a3)
    f1, s1 = stencils(b1, a1, a2, a3, a4)
    g1, t1 = stencils(b3, b2, b1, a1, a2)
    g2, t2 = stencils(b4, b3, b2, b1, a1)
    first_sum = sign * (g1 + ROOTS[0] * g2) + other[4:5]
    second_sum = t1 + ROOTS[1] * t2 + other[5:6]
    return (sign * f0, sign * f1, first_sum), (s0, s1, second_sum)


def wall_rows(own, sign):
    a1, a2, a3, a4 = layers(own, sign > 0)
    first = (sign * 0.5 * (4.0 * a2 - 3.0 * a1 - a3), sign * 0.75 * (a3 - a1), own[4:5])
    second = (2.0 * a1 - 5.0 * a2 + 4.0 * a3 - a4, 1.2 * (a3 - 2.0 * a2 + a1), own[5:6])
    return first, second


def layers(packed, ascending):
    rows = [packed[k : k + 1] for k in range(4)]
    return rows if ascending else rows[::-1]


def weigh(weights, values):
    return weights[0] * values[0] + weights[1] * values[1] + weights[2] * values[2]


def edge_terms(own, other, sign, wall=None):
    rows = edge_rows(own, other, sign)
    at_wall = None if wall is None else wall_rows(own, sign)
    terms = []
    for system in range(2):
        spread, first = [weigh(weights, rows[system]) for weights in inner_weights(system)]
        if wall is not None:
            pair = [weigh(weights, at_wall[system]) for weights in wall_weights(system)]
            spread = jnp.where(wall, pair[0], spread)
            first = jnp.where(wall, pair[1], first)
        at = iota((TILE, own.shape[1]), 0)
        at = at if sign > 0 else TILE - 1 - at
        far = powers(ROOTS[system], at) * spread
        terms.append((jnp.where(at == 0, first, far), far))
    return terms


def edge_update(low, high, system, tile, tiles):
    step = ROOTS[system] ** TILE
    up, down = tile, tiles - 1 - tile
    from_low = low[0] if up == 0 else low[1] * float(step**up)
    from_high = high[0] if down == 0 else high[1] * float(step**down)
    return from_low + from_high


def final_kernel(
    field, bulk, slope, bend, ye_own, xo_own, yo_own, xe_own, ye, xo, yo, xe, out
):
    slabs, rows, lanes = field.shape
    y_at, y_count = lax.axis_index("gy"), lax.axis_size("gy")
    x_even = lax.rem(lax.axis_index("gx"), 2) == 0
    y_even = lax.rem(y_at, 2) == 0
    count = slabs * rows
    pick = lambda flag, one, two: jnp.where(flag, one[...], two[...])
    pick_y = lambda flag, one, two: jnp.where(flag, one[:, :count], two[:, :count])
    low = edge_terms(pick_y(y_even, yo_own, ye_own), pick_y(y_even, yo, ye), 1.0, y_at == 0)
    high = edge_terms(
        pick_y(y_even, ye_own, yo_own), pick_y(y_even, ye, yo), -1.0, y_at == y_count - 1
    )
    tiles = lanes // TILE
    y_term = []
    for tile in range(tiles):
        place = slice(tile * TILE, (tile + 1) * TILE)
        one, two = [edge_update(low[k], high[k], k, tile, tiles) for k in range(2)]
        y_term.append(slope[place, :] * one + bend[place, :1] * two)
    y_term = jnp.transpose(jnp.concatenate(y_term, axis=0))
    low = edge_terms(pick(x_even, xo_own, xe_own), pick(x_even, xo, xe), 1.0)
    high = edge_terms(pick(x_even, xe_own, xo_own), pick(x_even, xe, xo), -1.0)
    tiles = rows // TILE
    for tile in range(tiles):
        one, two = [edge_update(low[k], high[k], k, tile, tiles) for k in range(2)]
        for s in range(slabs):
            place = slice(tile * TILE, (tile + 1) * TILE)
            part = slice(s * lanes, (s + 1) * lanes)
            turned = y_term[s * rows + tile * TILE : s * rows + (tile + 1) * TILE]
            x_term = VISCOSITY * two[:, part] - field[s // 3 * 3, place] * one[:, part]
            out[s, place] = bulk[s, place] + x_term + turned


def exchange_pairs(x_count, y_count):
    at = lambda x, y: x * y_count + y
    x_even = lambda x: x ^ 1
    x_odd = lambda x: (x + 1) % x_count if x % 2 else (x - 1) % x_count
    cells = [(x, y) for x in range(x_count) for y in range(y_count)]
    xe = [(at(x, y), at(x_even(x), y)) for x, y in cells]
    xo = [(at(x, y), at(x_odd(x), y)) for x, y in cells]
    ye = [(at(x, y), at(x, y ^ 1)) for x, y in cells]
    yo = [
        (at(x, y), at(x_even(x), y) if y in (0, y_count - 1) else at(x, y + 1 if y % 2 else y - 1))
        for x, y in cells
    ]
    return ye, xo, yo, xe


def call(kernel, outs, name, flops):
    vmem = pl.BlockSpec(memory_space=pltpu.VMEM)
    many = isinstance(outs, list)
    return lambda *args: pl.pallas_call(
        kernel,
        out_shape=outs,
        in_specs=[vmem] * len(args),
        out_specs=[vmem] * len(outs) if many else vmem,
        cost_estimate=pl.CostEstimate(flops=flops, bytes_accessed=10**6, transcendentals=0),
        compiler_params=pltpu.CompilerParams(vmem_limit_bytes=8 * 2**20),
        name=name,
    )(*args)


def shards(velocity, stretch, second_metric):
    planes, comps, rows, lanes = velocity.shape
    slabs = planes * comps
    x_count, y_count = lax.axis_size("gx"), lax.axis_size("gy")
    field = velocity.reshape(slabs, rows, lanes)
    stretch = stretch.reshape(y_count, lanes)
    metric = second_metric.reshape(y_count, lanes)

    shape = lambda *dims: jax.ShapeDtypeStruct(dims, jnp.float32)
    send = shape(8, slabs * max(lanes, rows))
    own = call(send_kernel, [send] * 4, "sends", 10**6)(field)
    pairs = exchange_pairs(x_count, y_count)
    moved = [lax.ppermute(value, ("gx", "gy"), way) for value, way in zip(own, pairs)]
    block = shape(slabs, rows, lanes)
    bulk = call(bulk_kernel, [block, shape(lanes, slabs * rows), shape(lanes, lanes)], "bulk", 10**8)(
        field, stretch, metric
    )
    out = call(final_kernel, block, "final", 10**7)(field, *bulk, *own, *moved)
    return out.reshape(planes, comps, rows, lanes)


def solution(mesh):
    return jax.shard_map(
        shards,
        mesh=mesh,
        in_specs=(P(None, None, "gx", "gy"), P(), P()),
        out_specs=P(None, None, "gx", "gy"),
        check_vma=False,
    )
```

```python
import jax
import jax.numpy as jnp
import numpy as np
from jax import lax
from jax.experimental import pallas as pl
from jax.experimental.pallas import tpu as pltpu
from jax.sharding import PartitionSpec as P

VISCOSITY = 0.5
COEFS = (1.0 / 3.0, 2.0 / 11.0)
WALL_COEFS = (1.0 / 4.0, 1.0 / 10.0)
HIGHEST = lax.Precision.HIGHEST
TILE = 8
ROUNDS = ("eeoe", "o11o", "1oe1", "2222")


def decay(coef):
    root = (-1.0 + np.sqrt(1.0 - 4.0 * coef * coef)) / (2.0 * coef)
    return float(root), float(1.0 / (1.0 + 2.0 * coef * root))


ROOTS = tuple(decay(coef)[0] for coef in COEFS)


def inner_weights(system):
    root, gain = decay(COEFS[system])
    return (gain, gain / root, gain * root), (gain, gain * root, gain * root)


def wall_weights(system):
    root, gain = decay(COEFS[system])
    size = 96
    band = np.full(size, COEFS[system])
    band[0], band[1] = 0.0, WALL_COEFS[system]
    matrix = np.eye(size) + np.diag(band[:-1], 1) + np.diag(band[1:], -1)
    inverse = np.linalg.solve(matrix, np.eye(size)[:, :3])
    spread = (inverse[:2, 2] - gain * root ** np.abs(np.arange(2) - 2.0)) / root**2
    columns = np.stack([inverse[:2, 0], inverse[:2, 1], spread], axis=1)
    return tuple(map(float, columns[1] / root)), tuple(map(float, columns[0]))


def iota(shape, axis):
    return lax.broadcasted_iota(jnp.int32, shape, axis)


def powers(root, exponent):
    size = jnp.exp(exponent.astype(jnp.float32) * float(np.log(-root)))
    return jnp.where(lax.rem(exponent, 2) == 0, size, -size)


def stencils(minus_two, minus_one, centre, plus_one, plus_two):
    first = 7.0 / 9.0 * (plus_one - minus_one) + 1.0 / 36.0 * (plus_two - minus_two)
    second = 12.0 / 11.0 * (plus_one - 2.0 * centre + minus_one) + 3.0 / 44.0 * (
        plus_two - 2.0 * centre + minus_two
    )
    return first, second


def right_sides(lines):
    turn = lambda steps: pltpu.roll(lines, steps % lines.shape[0], 0)
    at = iota(lines.shape, 0)
    inner = (at >= 2) & (at < lines.shape[0] - 2)
    parts = stencils(turn(2), turn(1), lines, turn(-1), turn(-2))
    return [jnp.where(inner, part, 0.0) for part in parts]


def edge_sums(part, root):
    rows, lanes = part.shape
    tiles = [part[k : k + TILE] for k in range(0, rows, TILE)]
    step = float(root**TILE)
    low, high = tiles[-1], tiles[0]
    for tile in tiles[-2::-1]:
        low = low * step + tile
    for tile in tiles[1:]:
        high = high * step + tile
    at = iota((TILE, lanes), 0)
    low = low * powers(root, at)
    high = high * powers(root, TILE - 1 - at)
    return jnp.sum(low, axis=0, keepdims=True), jnp.sum(high, axis=0, keepdims=True)


def own_edges(lines):
    rows = lines.shape[0]
    sums = [edge_sums(part, root) for part, root in zip(right_sides(lines), ROOTS)]
    low = [lines[k : k + 1] for k in range(4)], [sums[0][0], sums[1][0]]
    high = [lines[rows - 1 - k : rows - k] for k in range(4)], [sums[0][1], sums[1][1]]
    return low, high


def sent_rows(layers, sums, sign):
    b1, b2, b3, b4 = layers
    d2, d3, d4 = b2 - b1, b3 - b1, b4 - b1
    one, two = ROOTS
    first = 7.0 / 9.0 * (d2 + one * d3) + 1.0 / 36.0 * (d3 + one * d4)
    second = 12.0 / 11.0 * (d2 + two * (d3 - 2.0 * d2)) + 3.0 / 44.0 * (d3 + two * (d4 - 2.0 * d2))
    return [b1, b2, sums[0] - sign * first, sums[1] + second]


def received_sums(layers, received, sign):
    a1, a2 = layers[0] - received[0], layers[1] - received[0]
    one, two = ROOTS
    first = 7.0 / 9.0 * a1 + 1.0 / 36.0 * (a2 + one * a1)
    second = 12.0 / 11.0 * a1 + 3.0 / 44.0 * (a2 + two * a1)
    return received[2] + sign * first, received[3] + second


def turned(field):
    slabs, rows, lanes = field.shape
    fill = -(slabs * rows) % lanes
    lines = field.reshape(slabs * rows, lanes)
    if fill:
        lines = jnp.concatenate([lines, jnp.zeros((fill, lanes), jnp.float32)], axis=0)
    return jnp.transpose(lines)


def beyond(way, kind):
    return kind ^ 2 if way in "eo" else kind ^ 1


def arrival_rounds(way):
    return [
        next(k for k, ways in enumerate(ROUNDS) if ways[beyond(way, kind)] == way)
        for kind in range(4)
    ]


def by_kind(options):
    x_even = lax.rem(lax.axis_index("gx"), 2) == 0
    y_even = lax.rem(lax.axis_index("gy"), 2) == 0
    choose = lambda flag, one, two: one if one is two else jnp.where(flag, one, two)
    return choose(
        x_even, choose(y_even, options[0], options[1]), choose(y_even, options[2], options[3])
    )


def sends(edges, even, rows):
    low = [sent_rows(*at_low, -1.0) for at_low, _ in edges]
    high = [sent_rows(*at_high, 1.0) for _, at_high in edges]
    fill = rows - 4 * len(edges)
    fill = [jnp.zeros((fill, low[0][0].shape[1]), jnp.float32)] if fill else []
    from_low = jnp.concatenate([rows_of[k] for k in range(4) for rows_of in low] + fill, axis=0)
    from_high = jnp.concatenate([rows_of[k] for k in range(4) for rows_of in high] + fill, axis=0)
    return jnp.where(even, from_high, from_low), jnp.where(even, from_low, from_high)


def send_kernel(field, *outs):
    *outs, y_own = outs
    slabs, _, lanes = field.shape
    x_even = lax.rem(lax.axis_index("gx"), 2) == 0
    y_even = lax.rem(lax.axis_index("gy"), 2) == 0
    rows = outs[0].shape[0]
    lines = turned(field[...])
    edges = [own_edges(lines[:, k : k + lanes]) for k in range(0, lines.shape[1], lanes)]
    sent = {}
    sent["1"], sent["2"] = sends(edges, y_even, rows)
    for side in range(2):
        for k in range(6):
            values = [(edge[side][0] + edge[side][1])[k] for edge in edges]
            y_own[6 * side + k, : len(values)] = jnp.concatenate(values, axis=0)
    edges = [own_edges(field[s]) for s in range(slabs)]
    sent["e"], sent["o"] = sends(edges, x_even, rows)
    for out, ways in zip(outs, ROUNDS):
        out[...] = by_kind([sent[way] for way in ways])


def inverse_matrix(system, size):
    root, gain = decay(COEFS[system])
    return gain * powers(root, jnp.abs(iota((size, size), 0) - iota((size, size), 1)))


def solve(matrix, right_side):
    return jnp.dot(matrix, right_side, precision=HIGHEST, preferred_element_type=jnp.float32)


def bulk_kernel(field, stretch, metric, out, slope_turned, bend_turned, x_own):
    slabs, rows, lanes = field.shape
    position = pl.ds(lax.axis_index("gy"), 1)
    inv = 1.0 / stretch[position, :]
    curve = VISCOSITY * metric[position, :] * inv * inv * inv
    bend = jnp.transpose(jnp.broadcast_to(VISCOSITY * inv * inv, (lanes, lanes)))
    bend_turned[...] = bend
    slope = [-(field[plane * 3 + 1] * inv + curve) for plane in range(slabs // 3)]
    slope = turned(jnp.stack([part for part in slope for _ in range(3)], axis=0))
    slope_turned[...] = slope
    first, second = right_sides(turned(field[...]))
    y_term = slope * solve(inverse_matrix(0, lanes), first)
    y_term += bend[:, :1] * solve(inverse_matrix(1, lanes), second)
    y_term = jnp.transpose(y_term)
    matrices = [inverse_matrix(system, rows) for system in range(2)]
    for s in range(slabs):
        first, second = right_sides(field[s])
        x_term = VISCOSITY * solve(matrices[1], second) - field[s // 3 * 3] * solve(matrices[0], first)
        out[s] = x_term + y_term[s * rows : (s + 1) * rows]
        for k in range(4):
            x_own[k, s : s + 1] = field[s, k : k + 1]
            x_own[4 + k, s : s + 1] = field[s, rows - 1 - k : rows - k]


def edge_rows(own, received, sign):
    a1, a2, a3, a4 = own
    b1, b2 = received[:2]
    f0, s0 = stencils(b2, b1, a1, a2, a3)
    f1, s1 = stencils(b1, a1, a2, a3, a4)
    first_sum, second_sum = received_sums(own, received, sign)
    return (sign * f0, sign * f1, first_sum), (s0, s1, second_sum)


def wall_rows(own, sums, sign):
    a1, a2, a3, a4 = own
    first = (sign * 0.5 * (4.0 * a2 - 3.0 * a1 - a3), sign * 0.75 * (a3 - a1), sums[0])
    second = (2.0 * a1 - 5.0 * a2 + 4.0 * a3 - a4, 1.2 * (a3 - 2.0 * a2 + a1), sums[1])
    return first, second


def weigh(weights, values):
    return weights[0] * values[0] + weights[1] * values[1] + weights[2] * values[2]


def edge_numbers(own, received, sign, wall=None, sums=None):
    rows = edge_rows(own, received, sign)
    at_wall = None if wall is None else wall_rows(own, sums, sign)
    numbers = []
    for system in range(2):
        pair = [weigh(weights, rows[system]) for weights in inner_weights(system)]
        if wall is not None:
            other = [weigh(weights, at_wall[system]) for weights in wall_weights(system)]
            pair = [jnp.where(wall, there, here) for there, here in zip(other, pair)]
        numbers.append(pair)
    return numbers


def edge_tiles(pair, root, sign):
    at = iota((TILE, pair[0].shape[1]), 0)
    at = at if sign > 0 else TILE - 1 - at
    far = powers(root, at) * pair[0]
    return jnp.where(at == 0, pair[1], far), far


def line_tiles(numbers, line, sign):
    lines = [[part[line : line + 1] for part in pair] for pair in numbers]
    return [edge_tiles(pair, root, sign) for pair, root in zip(lines, ROOTS)]


def received(way, moved, groups):
    rounds = arrival_rounds(way)
    numbers = []
    for k in range(4):
        values = [part[k * groups : (k + 1) * groups, :] for part in moved]
        numbers.append(by_kind([values[at] for at in rounds]))
    return numbers


def select(flag, one, two):
    return [jnp.where(flag, there, here) for there, here in zip(one, two)]


def edge_update(low, high, root, tile, tiles):
    step = root**TILE
    up, down = tile, tiles - 1 - tile
    from_low = low[0] if up == 0 else low[1] * float(step**up)
    from_high = high[0] if down == 0 else high[1] * float(step**down)
    return from_low + from_high


def final_kernel(
    field, bulk, slope, bend, x_own, y_own, *refs
):
    *moved, out, block, sems = refs
    slabs, rows, lanes = field.shape
    y_at, y_count = lax.axis_index("gy"), lax.axis_size("gy")
    x_even = lax.rem(lax.axis_index("gx"), 2) == 0
    y_even = lax.rem(y_at, 2) == 0
    groups = slope.shape[1] // lanes
    own = [y_own[k, :groups] for k in range(12)]
    even, odd = [received(way, moved, groups) for way in "12"]
    from_low, from_high = select(y_even, odd, even), select(y_even, even, odd)
    low = edge_numbers(own[:4], from_low, 1.0, y_at == 0, own[4:6])
    high = edge_numbers(own[6:10], from_high, -1.0, y_at == y_count - 1, own[10:])
    tiles = lanes // TILE
    y_term = []
    for group in range(groups):
        at_low, at_high = line_tiles(low, group, 1.0), line_tiles(high, group, -1.0)
        part = slice(group * lanes, (group + 1) * lanes)
        column = []
        for tile in range(tiles):
            place = slice(tile * TILE, (tile + 1) * TILE)
            one, two = [edge_update(at_low[k], at_high[k], ROOTS[k], tile, tiles) for k in range(2)]
            column.append(slope[place, part] * one + bend[place, :] * two)
        y_term.append(jnp.transpose(jnp.concatenate(column, axis=0)))
    y_term = jnp.concatenate(y_term, axis=0)
    own = [x_own[k, :slabs] for k in range(8)]
    even, odd = [received(way, moved, slabs) for way in "eo"]
    low = edge_numbers(own[:4], select(x_even, odd, even), 1.0)
    high = edge_numbers(own[4:], select(x_even, even, odd), -1.0)
    tiles = rows // TILE
    copies = []
    for s in range(slabs):
        at_low, at_high = line_tiles(low, s, 1.0), line_tiles(high, s, -1.0)
        for tile in range(tiles):
            place = slice(tile * TILE, (tile + 1) * TILE)
            one, two = [edge_update(at_low[k], at_high[k], ROOTS[k], tile, tiles) for k in range(2)]
            turned = y_term[s * rows + tile * TILE : s * rows + (tile + 1) * TILE]
            x_term = VISCOSITY * two - field[s // 3 * 3, place] * one
            block[s, place] = bulk[s, place] + x_term + turned
        copies.append(pltpu.make_async_copy(block.at[s], out.at[s], sems.at[s]))
        copies[-1].start()
    for copy in copies:
        copy.wait()


def partner(way, x, y, x_count, y_count):
    if way == "2" and y in (0, y_count - 1):
        way = "e"
    if way in "eo":
        step = 1 if (x % 2 == 0) == (way == "e") else -1
        return (x + step) % x_count, y
    return x, y + (1 if (y % 2 == 0) == (way == "1") else -1)


def exchange_pairs(ways, x_count, y_count):
    at = lambda x, y: x * y_count + y
    return [
        (at(x, y), at(*partner(ways[x % 2 * 2 + y % 2], x, y, x_count, y_count)))
        for x in range(x_count)
        for y in range(y_count)
    ]


def call(kernel, outs, name, flops, out_space=pltpu.VMEM, scratch=()):
    vmem = pl.BlockSpec(memory_space=pltpu.VMEM)
    return lambda *args: pl.pallas_call(
        kernel,
        out_shape=outs,
        in_specs=[vmem] * len(args),
        out_specs=[pl.BlockSpec(memory_space=out_space)] * len(outs),
        scratch_shapes=scratch,
        cost_estimate=pl.CostEstimate(flops=flops, bytes_accessed=10**6, transcendentals=0),
        compiler_params=pltpu.CompilerParams(vmem_limit_bytes=8 * 2**20),
        name=name,
    )(*args)


def shards(velocity, stretch, second_metric):
    planes, comps, rows, lanes = velocity.shape
    slabs = planes * comps
    x_count, y_count = lax.axis_size("gx"), lax.axis_size("gy")
    field = velocity.reshape(slabs, rows, lanes)
    stretch = stretch.reshape(y_count, lanes)
    metric = second_metric.reshape(y_count, lanes)

    shape = lambda *dims: jax.ShapeDtypeStruct(dims, jnp.float32)
    groups = -(-slabs * rows // lanes)
    send = shape(4 * max(slabs, groups), lanes)
    *sent, y_own = call(send_kernel, [send] * len(ROUNDS) + [shape(12, TILE, lanes)], "sends", 10**6)(field)
    moved = [
        lax.ppermute(value, ("gx", "gy"), exchange_pairs(ways, x_count, y_count))
        for value, ways in zip(sent, ROUNDS)
    ]
    block = shape(slabs, rows, lanes)
    *bulk, x_own = call(
        bulk_kernel,
        [block, shape(lanes, groups * lanes), shape(lanes, lanes), shape(8, TILE, lanes)],
        "bulk",
        10**8,
    )(field, stretch, metric)
    (out,) = call(
        final_kernel,
        [block],
        "final",
        10**7,
        pl.ANY,
        [pltpu.VMEM(block.shape, jnp.float32), pltpu.SemaphoreType.DMA((slabs,))],
    )(field, *bulk, x_own, y_own, *moved)
    return out.reshape(planes, comps, rows, lanes)


def solution(mesh):
    return jax.shard_map(
        shards,
        mesh=mesh,
        in_specs=(P(None, None, "gx", "gy"), P(), P()),
        out_specs=P(None, None, "gx", "gy"),
        check_vma=False,
    )
```

```python
import jax
import jax.numpy as jnp
import numpy as np
from jax import lax
from jax.experimental import pallas as pl
from jax.experimental.pallas import tpu as pltpu
from jax.sharding import PartitionSpec as P

VISCOSITY = 0.5
COEFS = (1.0 / 3.0, 2.0 / 11.0)
WALL_COEFS = (1.0 / 4.0, 1.0 / 10.0)
HIGHEST = lax.Precision.HIGHEST
TILE = 8
WAYS = "eo12"
ROUNDS = (
    "2oeo22eooe22oeo2",
    "o211oo2e11ooe22o",
    "1eoee1o2eo1e2oe1",
    "e1221e1122e1111e",
)


def decay(coef):
    root = (-1.0 + np.sqrt(1.0 - 4.0 * coef * coef)) / (2.0 * coef)
    return float(root), float(1.0 / (1.0 + 2.0 * coef * root))


ROOTS = tuple(decay(coef)[0] for coef in COEFS)


def inner_weights(system):
    root, gain = decay(COEFS[system])
    return (gain, gain / root, gain * root), (gain, gain * root, gain * root)


def wall_weights(system):
    root, gain = decay(COEFS[system])
    size = 96
    band = np.full(size, COEFS[system])
    band[0], band[1] = 0.0, WALL_COEFS[system]
    matrix = np.eye(size) + np.diag(band[:-1], 1) + np.diag(band[1:], -1)
    inverse = np.linalg.solve(matrix, np.eye(size)[:, :3])
    spread = (inverse[:2, 2] - gain * root ** np.abs(np.arange(2) - 2.0)) / root**2
    columns = np.stack([inverse[:2, 0], inverse[:2, 1], spread], axis=1)
    return tuple(map(float, columns[1] / root)), tuple(map(float, columns[0]))


def iota(shape, axis):
    return lax.broadcasted_iota(jnp.int32, shape, axis)


def powers(root, exponent):
    size = jnp.exp(exponent.astype(jnp.float32) * float(np.log(-root)))
    return jnp.where(lax.rem(exponent, 2) == 0, size, -size)


def stencils(minus_two, minus_one, centre, plus_one, plus_two):
    first = 7.0 / 9.0 * (plus_one - minus_one) + 1.0 / 36.0 * (plus_two - minus_two)
    second = 12.0 / 11.0 * (plus_one - 2.0 * centre + minus_one) + 3.0 / 44.0 * (
        plus_two - 2.0 * centre + minus_two
    )
    return first, second


def right_sides(lines):
    turn = lambda steps: pltpu.roll(lines, steps % lines.shape[0], 0)
    at = iota(lines.shape, 0)
    inner = (at >= 2) & (at < lines.shape[0] - 2)
    parts = stencils(turn(2), turn(1), lines, turn(-1), turn(-2))
    return [jnp.where(inner, part, 0.0) for part in parts]


def tile_sums(part, root):
    rows, lanes = part.shape
    tiles = [part[k : k + TILE] for k in range(0, rows, TILE)]
    step = float(root**TILE)
    low, high = tiles[-1], tiles[0]
    for tile in tiles[-2::-1]:
        low = low * step + tile
    for tile in tiles[1:]:
        high = high * step + tile
    at = iota((TILE, lanes), 0)
    low = low * powers(root, at)
    high = high * powers(root, TILE - 1 - at)
    return jnp.sum(low, axis=0, keepdims=True), jnp.sum(high, axis=0, keepdims=True)


def difference_sums(lines):
    rows = lines.shape[0]
    at = iota(lines.shape, 0)
    first = jnp.where(at == rows - 1, 0.0, pltpu.roll(lines, rows - 1, 0) - lines)
    second = jnp.where((at == 0) | (at == rows - 1), 0.0, first - pltpu.roll(first, 1, 0))
    return *tile_sums(first, ROOTS[0]), *tile_sums(second, ROOTS[1])


def right_side_sums(layers, sums, rows):
    (one, two), size = ROOTS, rows
    steps = [[line[k + 1] - line[k] for k in range(3)] for line in layers]
    bends = [[line[k + 1] - line[k] for k in range(2)] for line in steps]
    near, far = 7.0 / 9.0 + 1.0 / 36.0, 1.0 / 36.0
    mid, side = 12.0 / 11.0 + 6.0 / 44.0, 3.0 / 44.0
    result = []
    for end in range(2):
        d0, d1, d2 = steps[end]
        z0, z1, z2 = [-step for step in steps[1 - end]]
        e1, e2 = bends[end]
        y1, y2 = bends[1 - end]
        total = sums[0] if end == 0 else sums[1] * float(-1.0 / one)
        last0, last1, last2 = [z * float(one ** (size - 2 - k)) for k, z in enumerate((z0, z1, z2))]
        first = (
            near * (total - d0 - one * d1 - last0)
            + (near * one) * (total - d0 - last0 - last1)
            + (far / one) * (total - d0 - one * d1 - one * one * d2)
            + (far * one * one) * (total - last0 - last1 - last2)
        )
        total = sums[2 + end]
        last1, last2 = y1 * float(two ** (size - 2)), y2 * float(two ** (size - 3))
        second = (
            mid * (total - two * e1 - last1)
            + (side / two) * (total - two * e1 - two * two * e2)
            + (side * two) * (total - last1 - last2)
        )
        result.append((first if end == 0 else -first, second))
    return result


def sent_rows(layers, sums, sign):
    b1, b2, b3, b4 = layers
    d2, d3, d4 = b2 - b1, b3 - b1, b4 - b1
    one, two = ROOTS
    first = 7.0 / 9.0 * (d2 + one * d3) + 1.0 / 36.0 * (d3 + one * d4)
    second = 12.0 / 11.0 * (d2 + two * (d3 - 2.0 * d2)) + 3.0 / 44.0 * (d3 + two * (d4 - 2.0 * d2))
    return [b1, b2, sums[0] - sign * first, sums[1] + second]


def received_sums(layers, received, sign):
    a1, a2 = layers[0] - received[0], layers[1] - received[0]
    one, two = ROOTS
    first = 7.0 / 9.0 * a1 + 1.0 / 36.0 * (a2 + one * a1)
    second = 12.0 / 11.0 * a1 + 3.0 / 44.0 * (a2 + two * a1)
    return received[2] + sign * first, received[3] + second


def turned(field):
    slabs, rows, lanes = field.shape
    fill = -(slabs * rows) % lanes
    lines = field.reshape(slabs * rows, lanes)
    if fill:
        lines = jnp.concatenate([lines, jnp.zeros((fill, lanes), jnp.float32)], axis=0)
    return jnp.transpose(lines)


def kind_of(x, y):
    return 8 * (x % 2) + 4 * (x // 2 % 2) + 2 * (y % 2) + y // 2 % 2


def beyond(way, kind):
    return kind ^ {"e": 8, "o": 12, "1": 2, "2": 3}[way]


def arrival_rounds(way):
    return [
        next(k for k, ways in enumerate(ROUNDS) if ways[beyond(way, kind)] == way)
        for kind in range(16)
    ]


def by_kind(numbers, options):
    packed = np.int64(sum(number << 2 * kind for kind, number in enumerate(numbers)))
    kind = kind_of(lax.axis_index("gx"), lax.axis_index("gy"))
    number = lax.shift_right_logical(jnp.int32(packed.astype(np.int32)), 2 * kind) & 3
    first, *others = sorted(set(numbers))
    chosen = options[first]
    for other in others:
        chosen = jnp.where(number == other, options[other], chosen)
    return chosen


def ends_of(groups):
    rows = groups[0].shape[0]
    stack = lambda values: jnp.concatenate(values, axis=0)
    layers = [
        [stack([group[at : at + 1] for group in groups]) for at in range(4)],
        [stack([group[rows - 1 - at : rows - at] for group in groups]) for at in range(4)],
    ]
    sums = [stack(values) for values in zip(*[difference_sums(group) for group in groups])]
    return layers, right_side_sums(layers, sums, rows)


def sends(layers, sums, even):
    low = sent_rows(layers[0], sums[0], -1.0)
    high = sent_rows(layers[1], sums[1], 1.0)
    return select(even, high, low), select(even, low, high)


def send_kernel(field, stretch, metric, _, *refs):
    *outs, metrics, x_own, y_own = refs
    metrics[...] = metric_rows(stretch, metric)
    slabs, _, lanes = field.shape
    x_even = lax.rem(lax.axis_index("gx"), 2) == 0
    y_even = lax.rem(lax.axis_index("gy"), 2) == 0
    groups = [field[s] for s in range(slabs)]
    layers, sums = ends_of(groups)
    sent = dict(zip("eo", sends(layers, sums, x_even)))
    for k, layer in enumerate(layers[0] + layers[1]):
        x_own[k, :slabs] = layer
    lines = turned(field[...])
    layers, sums = ends_of([lines[:, k : k + lanes] for k in range(0, lines.shape[1], lanes)])
    sent.update(zip("12", sends(layers, sums, y_even)))
    for k, values in enumerate([*layers[0], *sums[0], *layers[1], *sums[1]]):
        y_own[k, : values.shape[0]] = values
    for out, ways in zip(outs, ROUNDS):
        count = out.shape[0] // 4
        options = {}
        for number, way in enumerate(WAYS):
            if way in ways:
                fill = jnp.zeros((count - sent[way][0].shape[0], lanes), jnp.float32)
                parts = [part for value in sent[way] for part in (value, fill) if part.shape[0]]
                options[number] = jnp.concatenate(parts, axis=0)
        out[...] = by_kind([WAYS.index(way) for way in ways], options)


def inverse_matrix(system, size):
    root, gain = decay(COEFS[system])
    return gain * powers(root, jnp.abs(iota((size, size), 0) - iota((size, size), 1)))


def solve(matrix, right_side):
    return jnp.dot(matrix, right_side, precision=HIGHEST, preferred_element_type=jnp.float32)


def table_kernel(y_out, x_out):
    for system in range(2):
        y_out[system] = inverse_matrix(system, y_out.shape[1])
        x_out[system] = inverse_matrix(system, x_out.shape[1])


def metric_rows(stretch, metric):
    position = pl.ds(lax.axis_index("gy"), 1)
    inv = 1.0 / stretch[position, :]
    curve = VISCOSITY * metric[position, :] * inv * inv * inv
    fill = jnp.zeros((TILE - 3, inv.shape[1]), jnp.float32)
    return jnp.concatenate([inv, curve, VISCOSITY * inv * inv, fill], axis=0)


def bulk_kernel(field, metrics, y_matrix, x_matrix, out, slope_turned, bend_turned):
    slabs, rows, lanes = field.shape
    inv, curve, bend = metrics[0:1, :], metrics[1:2, :], metrics[2:3, :]
    bend = jnp.transpose(jnp.broadcast_to(bend, (lanes, lanes)))
    bend_turned[...] = bend
    slope = [-(field[plane * 3 + 1] * inv + curve) for plane in range(slabs // 3)]
    slope = turned(jnp.stack([part for part in slope for _ in range(3)], axis=0))
    slope_turned[...] = slope
    first, second = right_sides(turned(field[...]))
    y_term = slope * solve(y_matrix[0], first) + bend[:, :1] * solve(y_matrix[1], second)
    y_term = jnp.transpose(y_term)
    for s in range(slabs):
        first, second = right_sides(field[s])
        x_term = VISCOSITY * solve(x_matrix[1], second) - field[s // 3 * 3] * solve(x_matrix[0], first)
        out[s] = x_term + y_term[s * rows : (s + 1) * rows]


def edge_rows(own, received, sign):
    a1, a2, a3, a4 = own
    b1, b2 = received[:2]
    f0, s0 = stencils(b2, b1, a1, a2, a3)
    f1, s1 = stencils(b1, a1, a2, a3, a4)
    first_sum, second_sum = received_sums(own, received, sign)
    return (sign * f0, sign * f1, first_sum), (s0, s1, second_sum)


def wall_rows(own, sums, sign):
    a1, a2, a3, a4 = own
    first = (sign * 0.5 * (4.0 * a2 - 3.0 * a1 - a3), sign * 0.75 * (a3 - a1), sums[0])
    second = (2.0 * a1 - 5.0 * a2 + 4.0 * a3 - a4, 1.2 * (a3 - 2.0 * a2 + a1), sums[1])
    return first, second


def weigh(weights, values):
    return weights[0] * values[0] + weights[1] * values[1] + weights[2] * values[2]


def edge_numbers(own, received, sign, wall=None, sums=None):
    rows = edge_rows(own, received, sign)
    at_wall = None if wall is None else wall_rows(own, sums, sign)
    numbers = []
    for system in range(2):
        pair = [weigh(weights, rows[system]) for weights in inner_weights(system)]
        if wall is not None:
            other = [weigh(weights, at_wall[system]) for weights in wall_weights(system)]
            pair = [jnp.where(wall, there, here) for there, here in zip(other, pair)]
        numbers.append(pair)
    return numbers


def edge_tiles(pair, root, sign):
    at = iota((TILE, pair[0].shape[1]), 0)
    at = at if sign > 0 else TILE - 1 - at
    far = powers(root, at) * pair[0]
    return jnp.where(at == 0, pair[1], far), far


def line_tiles(numbers, line, sign):
    lines = [[part[line : line + 1] for part in pair] for pair in numbers]
    return [edge_tiles(pair, root, sign) for pair, root in zip(lines, ROOTS)]


def received(way, moved, groups):
    rounds = arrival_rounds(way)
    numbers = []
    for k in range(4):
        values = {
            at: moved[at][pl.ds(k * (moved[at].shape[0] // 4), groups), :] for at in set(rounds)
        }
        numbers.append(by_kind(rounds, values))
    return numbers


def select(flag, one, two):
    return [jnp.where(flag, there, here) for there, here in zip(one, two)]


def edge_update(low, high, root, tile, tiles):
    step = root**TILE
    up, down = tile, tiles - 1 - tile
    from_low = low[0] if up == 0 else low[1] * float(step**up)
    from_high = high[0] if down == 0 else high[1] * float(step**down)
    return from_low + from_high


def final_kernel(
    field, bulk, slope, bend, x_own, y_own, *refs
):
    *moved, out, block, sems = refs
    slabs, rows, lanes = field.shape
    y_at, y_count = lax.axis_index("gy"), lax.axis_size("gy")
    x_even = lax.rem(lax.axis_index("gx"), 2) == 0
    y_even = lax.rem(y_at, 2) == 0
    groups = slope.shape[1] // lanes
    own = [y_own[k, :groups] for k in range(12)]
    even, odd = [received(way, moved, groups) for way in "12"]
    from_low, from_high = select(y_even, odd, even), select(y_even, even, odd)
    low = edge_numbers(own[:4], from_low, 1.0, y_at == 0, own[4:6])
    high = edge_numbers(own[6:10], from_high, -1.0, y_at == y_count - 1, own[10:])
    tiles = lanes // TILE
    y_term = []
    for group in range(groups):
        at_low, at_high = line_tiles(low, group, 1.0), line_tiles(high, group, -1.0)
        part = slice(group * lanes, (group + 1) * lanes)
        column = []
        for tile in range(tiles):
            place = slice(tile * TILE, (tile + 1) * TILE)
            one, two = [edge_update(at_low[k], at_high[k], ROOTS[k], tile, tiles) for k in range(2)]
            column.append(slope[place, part] * one + bend[place, :] * two)
        y_term.append(jnp.transpose(jnp.concatenate(column, axis=0)))
    y_term = jnp.concatenate(y_term, axis=0)
    own = [x_own[k, :slabs] for k in range(8)]
    even, odd = [received(way, moved, slabs) for way in "eo"]
    low = edge_numbers(own[:4], select(x_even, odd, even), 1.0)
    high = edge_numbers(own[4:], select(x_even, even, odd), -1.0)
    tiles = rows // TILE
    copies = []
    for s in range(slabs):
        at_low, at_high = line_tiles(low, s, 1.0), line_tiles(high, s, -1.0)
        for tile in range(tiles):
            place = slice(tile * TILE, (tile + 1) * TILE)
            one, two = [edge_update(at_low[k], at_high[k], ROOTS[k], tile, tiles) for k in range(2)]
            turned = y_term[s * rows + tile * TILE : s * rows + (tile + 1) * TILE]
            x_term = VISCOSITY * two - field[s // 3 * 3, place] * one
            block[s, place] = bulk[s, place] + x_term + turned
        copies.append(pltpu.make_async_copy(block.at[s], out.at[s], sems.at[s]))
        copies[-1].start()
    for copy in copies:
        copy.wait()


def partner(way, x, y, x_count, y_count):
    if way == "2" and y in (0, y_count - 1):
        way = "e"
    if way in "eo":
        step = 1 if (x % 2 == 0) == (way == "e") else -1
        return (x + step) % x_count, y
    return x, y + (1 if (y % 2 == 0) == (way == "1") else -1)


def exchange_pairs(ways, x_count, y_count):
    at = lambda x, y: x * y_count + y
    return [
        (at(x, y), at(*partner(ways[kind_of(x, y)], x, y, x_count, y_count)))
        for x in range(x_count)
        for y in range(y_count)
    ]


def call(kernel, outs, name, flops, out_space=pltpu.VMEM, scratch=()):
    return lambda *args: pl.pallas_call(
        kernel,
        out_shape=outs,
        in_specs=[pl.BlockSpec(memory_space=pltpu.VMEM)] * len(args),
        out_specs=[pl.BlockSpec(memory_space=out_space)] * len(outs),
        scratch_shapes=scratch,
        cost_estimate=pl.CostEstimate(flops=flops, bytes_accessed=0, transcendentals=0),
        compiler_params=pltpu.CompilerParams(vmem_limit_bytes=8 * 2**20),
        name=name,
    )(*args)


def shards(velocity, stretch, second_metric):
    planes, comps, rows, lanes = velocity.shape
    slabs = planes * comps
    x_count, y_count = lax.axis_size("gx"), lax.axis_size("gy")
    stretch = stretch.reshape(y_count, lanes)
    metric = second_metric.reshape(y_count, lanes)
    shape = lambda *dims: jax.ShapeDtypeStruct(dims, jnp.float32)
    block = shape(slabs, rows, lanes)
    move = lambda value, ways: lax.ppermute(
        value, ("gx", "gy"), exchange_pairs(ways, x_count, y_count)
    )

    tables = call(table_kernel, [shape(2, lanes, lanes), shape(2, rows, rows)], "tables", 10**8)()
    field = velocity.reshape(slabs, rows, lanes)
    groups = -(-slabs * rows // lanes)
    send = shape(4 * max(slabs, groups), lanes)
    *sent, metrics, x_own, y_own = call(
        send_kernel,
        [send] * len(ROUNDS)
        + [shape(TILE, lanes), shape(8, TILE, lanes), shape(12, TILE, lanes)],
        "sends",
        10**6,
    )(field, stretch, metric, tables[1])
    moved = [move(value, ways) for value, ways in zip(sent, ROUNDS)]
    bulk = call(
        bulk_kernel, [block, shape(lanes, groups * lanes), shape(lanes, lanes)], "bulk", 10**8
    )(field, metrics, *tables)
    (out,) = call(
        final_kernel,
        [block],
        "final",
        10**7,
        pl.ANY,
        [pltpu.VMEM(block.shape, jnp.float32), pltpu.SemaphoreType.DMA((slabs,))],
    )(field, *bulk, x_own, y_own, *moved)
    return out.reshape(planes, comps, rows, lanes)


def solution(mesh):
    return jax.shard_map(
        shards,
        mesh=mesh,
        in_specs=(P(None, None, "gx", "gy"), P(), P()),
        out_specs=P(None, None, "gx", "gy"),
        check_vma=False,
    )
```

```python
import jax
import jax.numpy as jnp
import numpy as np
from jax import lax
from jax.experimental import pallas as pl
from jax.experimental.pallas import tpu as pltpu
from jax.sharding import PartitionSpec as P

VISCOSITY = 0.5
COEFS = (1.0 / 3.0, 2.0 / 11.0)
WALL_COEFS = (1.0 / 4.0, 1.0 / 10.0)
HIGHEST = lax.Precision.HIGHEST
TILE = 8
WAYS = "eo12"
ROUNDS = (
    "2oeo22eooe22oeo2",
    "o211oo2e11ooe22o",
    "1eoee1o2eo1e2oe1",
    "e1221e1122e1111e",
)


def decay(coef):
    root = (-1.0 + np.sqrt(1.0 - 4.0 * coef * coef)) / (2.0 * coef)
    return float(root), float(1.0 / (1.0 + 2.0 * coef * root))


ROOTS = tuple(decay(coef)[0] for coef in COEFS)


def inner_weights(system):
    root, gain = decay(COEFS[system])
    return (gain, gain / root, gain * root), (gain, gain * root, gain * root)


def wall_weights(system):
    root, gain = decay(COEFS[system])
    size = 96
    band = np.full(size, COEFS[system])
    band[0], band[1] = 0.0, WALL_COEFS[system]
    matrix = np.eye(size) + np.diag(band[:-1], 1) + np.diag(band[1:], -1)
    inverse = np.linalg.solve(matrix, np.eye(size)[:, :3])
    spread = (inverse[:2, 2] - gain * root ** np.abs(np.arange(2) - 2.0)) / root**2
    columns = np.stack([inverse[:2, 0], inverse[:2, 1], spread], axis=1)
    return tuple(map(float, columns[1] / root)), tuple(map(float, columns[0]))


def iota(shape, axis):
    return lax.broadcasted_iota(jnp.int32, shape, axis)


def powers(root, exponent):
    size = jnp.exp(exponent.astype(jnp.float32) * float(np.log(-root)))
    return jnp.where(lax.rem(exponent, 2) == 0, size, -size)


def stencils(minus_two, minus_one, centre, plus_one, plus_two):
    first = 7.0 / 9.0 * (plus_one - minus_one) + 1.0 / 36.0 * (plus_two - minus_two)
    second = 12.0 / 11.0 * (plus_one - 2.0 * centre + minus_one) + 3.0 / 44.0 * (
        plus_two - 2.0 * centre + minus_two
    )
    return first, second


def right_sides(lines):
    turn = lambda steps: pltpu.roll(lines, steps % lines.shape[0], 0)
    at = iota(lines.shape, 0)
    inner = (at >= 2) & (at < lines.shape[0] - 2)
    parts = stencils(turn(2), turn(1), lines, turn(-1), turn(-2))
    return [jnp.where(inner, part, 0.0) for part in parts]


def ramps(lanes):
    at = iota((TILE, lanes), 0)
    return [(powers(root, at), powers(root, TILE - 1 - at)) for root in ROOTS]


def difference_sums(lines, ramp):
    rows, lanes = lines.shape
    steps = pltpu.roll(lines, rows - 1, 0) - lines
    tiles = [steps[k : k + TILE] for k in range(0, rows, TILE)]
    tiles[-1] = jnp.where(iota((TILE, lanes), 0) == TILE - 1, 0.0, tiles[-1])
    sums = []
    for root, (up, down) in zip(ROOTS, ramp):
        step = float(root**TILE)
        low, high = tiles[-1], tiles[0]
        for tile in tiles[-2::-1]:
            low = low * step + tile
        for tile in tiles[1:]:
            high = high * step + tile
        sums.append(jnp.sum(low * up, axis=0, keepdims=True))
        sums.append(jnp.sum(high * down, axis=0, keepdims=True))
    return sums


def right_side_sums(layers, sums, rows):
    (one, two), size = ROOTS, rows
    steps = [[line[k + 1] - line[k] for k in range(3)] for line in layers]
    bends = [[line[k + 1] - line[k] for k in range(2)] for line in steps]
    near, far = 7.0 / 9.0 + 1.0 / 36.0, 1.0 / 36.0
    mid, side = 12.0 / 11.0 + 6.0 / 44.0, 3.0 / 44.0
    result = []
    for end in range(2):
        d0, d1, d2 = steps[end]
        z0, z1, z2 = [-step for step in steps[1 - end]]
        e1, e2 = bends[end]
        y1, y2 = bends[1 - end]
        total = sums[0] if end == 0 else sums[1] * float(-1.0 / one)
        last0, last1, last2 = [z * float(one ** (size - 2 - k)) for k, z in enumerate((z0, z1, z2))]
        first = (
            near * (total - d0 - one * d1 - last0)
            + (near * one) * (total - d0 - last0 - last1)
            + (far / one) * (total - d0 - one * d1 - one * one * d2)
            + (far * one * one) * (total - last0 - last1 - last2)
        )
        total = sums[2] if end == 0 else sums[3] * float(-1.0 / two)
        total = (1.0 - two) * total - d0 + z0 * float(two ** (size - 1))
        last1, last2 = y1 * float(two ** (size - 2)), y2 * float(two ** (size - 3))
        second = (
            mid * (total - two * e1 - last1)
            + (side / two) * (total - two * e1 - two * two * e2)
            + (side * two) * (total - last1 - last2)
        )
        result.append((first if end == 0 else -first, second))
    return result


def sent_rows(layers, sums, sign):
    b1, b2, b3, b4 = layers
    d2, d3, d4 = b2 - b1, b3 - b1, b4 - b1
    one, two = ROOTS
    first = 7.0 / 9.0 * (d2 + one * d3) + 1.0 / 36.0 * (d3 + one * d4)
    second = 12.0 / 11.0 * (d2 + two * (d3 - 2.0 * d2)) + 3.0 / 44.0 * (d3 + two * (d4 - 2.0 * d2))
    return [b1, b2, sums[0] - sign * first, sums[1] + second]


def received_sums(layers, received, sign):
    a1, a2 = layers[0] - received[0], layers[1] - received[0]
    one, two = ROOTS
    first = 7.0 / 9.0 * a1 + 1.0 / 36.0 * (a2 + one * a1)
    second = 12.0 / 11.0 * a1 + 3.0 / 44.0 * (a2 + two * a1)
    return received[2] + sign * first, received[3] + second


def turned(field):
    slabs, rows, lanes = field.shape
    fill = -(slabs * rows) % lanes
    lines = field.reshape(slabs * rows, lanes)
    if fill:
        lines = jnp.concatenate([lines, jnp.zeros((fill, lanes), jnp.float32)], axis=0)
    return jnp.transpose(lines)


def kind_of(x, y):
    return 8 * (x % 2) + 4 * (x // 2 % 2) + 2 * (y % 2) + y // 2 % 2


def beyond(way, kind):
    return kind ^ {"e": 8, "o": 12, "1": 2, "2": 3}[way]


def arrival_rounds(way):
    return [
        next(k for k, ways in enumerate(ROUNDS) if ways[beyond(way, kind)] == way)
        for kind in range(16)
    ]


def by_kind(numbers, options):
    packed = np.int64(sum(number << 2 * kind for kind, number in enumerate(numbers)))
    kind = kind_of(lax.axis_index("gx"), lax.axis_index("gy"))
    number = lax.shift_right_logical(jnp.int32(packed.astype(np.int32)), 2 * kind) & 3
    first, *others = sorted(set(numbers))
    chosen = options[first]
    for other in others:
        chosen = jnp.where(number == other, options[other], chosen)
    return chosen


def ends_of(groups, ramp):
    rows = groups[0].shape[0]
    stack = lambda values: jnp.concatenate(values, axis=0)
    layers = [
        [stack([group[at : at + 1] for group in groups]) for at in range(4)],
        [stack([group[rows - 1 - at : rows - at] for group in groups]) for at in range(4)],
    ]
    sums = [stack(values) for values in zip(*[difference_sums(group, ramp) for group in groups])]
    return layers, right_side_sums(layers, sums, rows)


def sends(layers, sums, even):
    low = sent_rows(layers[0], sums[0], -1.0)
    high = sent_rows(layers[1], sums[1], 1.0)
    return select(even, high, low), select(even, low, high)


def send_kernel(field, stretch, metric, _, *refs):
    *outs, metrics, x_own, y_own = refs
    metrics[...] = metric_rows(stretch, metric)
    slabs, _, lanes = field.shape
    x_even = lax.rem(lax.axis_index("gx"), 2) == 0
    y_even = lax.rem(lax.axis_index("gy"), 2) == 0
    groups = [field[s] for s in range(slabs)]
    ramp = ramps(lanes)
    layers, sums = ends_of(groups, ramp)
    sent = dict(zip("eo", sends(layers, sums, x_even)))
    for k, layer in enumerate(layers[0] + layers[1]):
        x_own[k, :slabs] = layer
    lines = turned(field[...])
    layers, sums = ends_of(
        [lines[:, k : k + lanes] for k in range(0, lines.shape[1], lanes)], ramp
    )
    sent.update(zip("12", sends(layers, sums, y_even)))
    for k, values in enumerate([*layers[0], *sums[0], *layers[1], *sums[1]]):
        y_own[k, : values.shape[0]] = values
    for out, ways in zip(outs, ROUNDS):
        count = out.shape[0] // 4
        options = {}
        for number, way in enumerate(WAYS):
            if way in ways:
                fill = jnp.zeros((count - sent[way][0].shape[0], lanes), jnp.float32)
                parts = [part for value in sent[way] for part in (value, fill) if part.shape[0]]
                options[number] = jnp.concatenate(parts, axis=0)
        out[...] = by_kind([WAYS.index(way) for way in ways], options)


def inverse_matrix(system, size):
    root, gain = decay(COEFS[system])
    return gain * powers(root, jnp.abs(iota((size, size), 0) - iota((size, size), 1)))


def solve(matrix, right_side):
    return jnp.dot(matrix, right_side, precision=HIGHEST, preferred_element_type=jnp.float32)


def table_kernel(y_out, x_out):
    for system in range(2):
        y_out[system] = inverse_matrix(system, y_out.shape[1])
        x_out[system] = inverse_matrix(system, x_out.shape[1])


def metric_rows(stretch, metric):
    position = pl.ds(lax.axis_index("gy"), 1)
    inv = 1.0 / stretch[position, :]
    curve = VISCOSITY * metric[position, :] * inv * inv * inv
    fill = jnp.zeros((TILE - 3, inv.shape[1]), jnp.float32)
    return jnp.concatenate([inv, curve, VISCOSITY * inv * inv, fill], axis=0)


def bulk_kernel(field, metrics, y_matrix, x_matrix, out, slope_turned, bend_turned):
    slabs, rows, lanes = field.shape
    inv, curve, bend = metrics[0:1, :], metrics[1:2, :], metrics[2:3, :]
    bend = jnp.transpose(jnp.broadcast_to(bend, (lanes, lanes)))
    bend_turned[...] = bend
    slope = [-(field[plane * 3 + 1] * inv + curve) for plane in range(slabs // 3)]
    slope = turned(jnp.stack([part for part in slope for _ in range(3)], axis=0))
    slope_turned[...] = slope
    first, second = right_sides(turned(field[...]))
    y_term = slope * solve(y_matrix[0], first) + bend[:, :1] * solve(y_matrix[1], second)
    y_term = jnp.transpose(y_term)
    for s in range(slabs):
        first, second = right_sides(field[s])
        x_term = VISCOSITY * solve(x_matrix[1], second) - field[s // 3 * 3] * solve(x_matrix[0], first)
        out[s] = x_term + y_term[s * rows : (s + 1) * rows]


def edge_rows(own, received, sign):
    a1, a2, a3, a4 = own
    b1, b2 = received[:2]
    f0, s0 = stencils(b2, b1, a1, a2, a3)
    f1, s1 = stencils(b1, a1, a2, a3, a4)
    first_sum, second_sum = received_sums(own, received, sign)
    return (sign * f0, sign * f1, first_sum), (s0, s1, second_sum)


def wall_rows(own, sums, sign):
    a1, a2, a3, a4 = own
    first = (sign * 0.5 * (4.0 * a2 - 3.0 * a1 - a3), sign * 0.75 * (a3 - a1), sums[0])
    second = (2.0 * a1 - 5.0 * a2 + 4.0 * a3 - a4, 1.2 * (a3 - 2.0 * a2 + a1), sums[1])
    return first, second


def weigh(weights, values):
    return weights[0] * values[0] + weights[1] * values[1] + weights[2] * values[2]


def edge_numbers(own, received, sign, wall=None, sums=None):
    rows = edge_rows(own, received, sign)
    at_wall = None if wall is None else wall_rows(own, sums, sign)
    numbers = []
    for system in range(2):
        pair = [weigh(weights, rows[system]) for weights in inner_weights(system)]
        if wall is not None:
            other = [weigh(weights, at_wall[system]) for weights in wall_weights(system)]
            pair = [jnp.where(wall, there, here) for there, here in zip(other, pair)]
        numbers.append(pair)
    return numbers


def edge_tiles(numbers, line, side, ramp):
    tiles = []
    for (spread, first), powers_of in zip(numbers, ramp):
        far = powers_of[side] * spread[line : line + 1]
        at_edge = iota(far.shape, 0) == (TILE - 1 if side else 0)
        tiles.append((jnp.where(at_edge, first[line : line + 1], far), far))
    return tiles


def received(way, moved, groups):
    rounds = arrival_rounds(way)
    numbers = []
    for k in range(4):
        values = {
            at: moved[at][pl.ds(k * (moved[at].shape[0] // 4), groups), :] for at in set(rounds)
        }
        numbers.append(by_kind(rounds, values))
    return numbers


def select(flag, one, two):
    return [jnp.where(flag, there, here) for there, here in zip(one, two)]


def edge_update(low, high, root, tile, tiles):
    parts = []
    for (near, far), steps in ((low, tile), (high, tiles - 1 - tile)):
        scale = float(root ** (TILE * steps))
        if abs(scale) > np.finfo(np.float32).tiny:
            parts.append(far * scale if steps else near)
    return sum(parts[1:], parts[0]) if parts else None


def final_kernel(
    field, bulk, slope, bend, x_own, y_own, *refs
):
    *moved, out, block, sems = refs
    slabs, rows, lanes = field.shape
    y_at, y_count = lax.axis_index("gy"), lax.axis_size("gy")
    x_even = lax.rem(lax.axis_index("gx"), 2) == 0
    y_even = lax.rem(y_at, 2) == 0
    groups = slope.shape[1] // lanes
    own = [y_own[k, :groups] for k in range(12)]
    even, odd = [received(way, moved, groups) for way in "12"]
    from_low, from_high = select(y_even, odd, even), select(y_even, even, odd)
    low = edge_numbers(own[:4], from_low, 1.0, y_at == 0, own[4:6])
    high = edge_numbers(own[6:10], from_high, -1.0, y_at == y_count - 1, own[10:])
    tiles, ramp = lanes // TILE, ramps(lanes)
    y_term = []
    for group in range(groups):
        at_low, at_high = edge_tiles(low, group, 0, ramp), edge_tiles(high, group, 1, ramp)
        part = slice(group * lanes, (group + 1) * lanes)
        column = []
        for tile in range(tiles):
            place = slice(tile * TILE, (tile + 1) * TILE)
            one, two = [edge_update(at_low[k], at_high[k], ROOTS[k], tile, tiles) for k in range(2)]
            term = slope[place, part] * one
            column.append(term if two is None else term + bend[place, :] * two)
        y_term.append(jnp.transpose(jnp.concatenate(column, axis=0)))
    y_term = jnp.concatenate(y_term, axis=0)
    own = [x_own[k, :slabs] for k in range(8)]
    even, odd = [received(way, moved, slabs) for way in "eo"]
    low = edge_numbers(own[:4], select(x_even, odd, even), 1.0)
    high = edge_numbers(own[4:], select(x_even, even, odd), -1.0)
    for _, second in (low, high):
        second[:] = [VISCOSITY * number for number in second]
    tiles = rows // TILE
    copies = []
    for s in range(slabs):
        at_low, at_high = edge_tiles(low, s, 0, ramp), edge_tiles(high, s, 1, ramp)
        for tile in range(tiles):
            place = slice(tile * TILE, (tile + 1) * TILE)
            one, two = [edge_update(at_low[k], at_high[k], ROOTS[k], tile, tiles) for k in range(2)]
            turned = y_term[s * rows + tile * TILE : s * rows + (tile + 1) * TILE]
            x_term = two - field[s // 3 * 3, place] * one
            block[s, place] = bulk[s, place] + x_term + turned
        copies.append(pltpu.make_async_copy(block.at[s], out.at[s], sems.at[s]))
        copies[-1].start()
    for copy in copies:
        copy.wait()


def partner(way, x, y, x_count, y_count):
    if way == "2" and y in (0, y_count - 1):
        way = "e"
    if way in "eo":
        step = 1 if (x % 2 == 0) == (way == "e") else -1
        return (x + step) % x_count, y
    return x, y + (1 if (y % 2 == 0) == (way == "1") else -1)


def exchange_pairs(ways, x_count, y_count):
    at = lambda x, y: x * y_count + y
    return [
        (at(x, y), at(*partner(ways[kind_of(x, y)], x, y, x_count, y_count)))
        for x in range(x_count)
        for y in range(y_count)
    ]


def call(kernel, outs, name, flops, out_space=pltpu.VMEM, scratch=()):
    return lambda *args: pl.pallas_call(
        kernel,
        out_shape=outs,
        in_specs=[pl.BlockSpec(memory_space=pltpu.VMEM)] * len(args),
        out_specs=[pl.BlockSpec(memory_space=out_space)] * len(outs),
        scratch_shapes=scratch,
        cost_estimate=pl.CostEstimate(flops=flops, bytes_accessed=0, transcendentals=0),
        compiler_params=pltpu.CompilerParams(vmem_limit_bytes=8 * 2**20),
        name=name,
    )(*args)


def shards(velocity, stretch, second_metric):
    planes, comps, rows, lanes = velocity.shape
    slabs = planes * comps
    x_count, y_count = lax.axis_size("gx"), lax.axis_size("gy")
    stretch = stretch.reshape(y_count, lanes)
    metric = second_metric.reshape(y_count, lanes)
    shape = lambda *dims: jax.ShapeDtypeStruct(dims, jnp.float32)
    block = shape(slabs, rows, lanes)
    move = lambda value, ways: lax.ppermute(
        value, ("gx", "gy"), exchange_pairs(ways, x_count, y_count)
    )

    tables = call(table_kernel, [shape(2, lanes, lanes), shape(2, rows, rows)], "tables", 10**8)()
    field = velocity.reshape(slabs, rows, lanes)
    groups = -(-slabs * rows // lanes)
    send = shape(4 * max(slabs, groups), lanes)
    *sent, metrics, x_own, y_own = call(
        send_kernel,
        [send] * len(ROUNDS)
        + [shape(TILE, lanes), shape(8, TILE, lanes), shape(12, TILE, lanes)],
        "sends",
        10**6,
    )(field, stretch, metric, tables[1])
    moved = [move(value, ways) for value, ways in zip(sent, ROUNDS)]
    bulk = call(
        bulk_kernel, [block, shape(lanes, groups * lanes), shape(lanes, lanes)], "bulk", 10**8
    )(field, metrics, *tables)
    (out,) = call(
        final_kernel,
        [block],
        "final",
        10**7,
        pl.ANY,
        [pltpu.VMEM(block.shape, jnp.float32), pltpu.SemaphoreType.DMA((slabs,))],
    )(field, *bulk, x_own, y_own, *moved)
    return out.reshape(planes, comps, rows, lanes)


def solution(mesh):
    return jax.shard_map(
        shards,
        mesh=mesh,
        in_specs=(P(None, None, "gx", "gy"), P(), P()),
        out_specs=P(None, None, "gx", "gy"),
        check_vma=False,
    )
```

```python
import jax
import jax.numpy as jnp
import numpy as np
from jax import lax
from jax.experimental import pallas as pl
from jax.experimental.pallas import tpu as pltpu
from jax.sharding import PartitionSpec as P

VISCOSITY = 0.5
COEFS = (1.0 / 3.0, 2.0 / 11.0)
WALL_COEFS = (1.0 / 4.0, 1.0 / 10.0)
HIGHEST = lax.Precision.HIGHEST
TILE = 8
WAYS = "eo12"
ROUNDS = (
    "2oeo22eooe22oeo2",
    "o211oo2e11ooe22o",
    "1eoee1o2eo1e2oe1",
    "e1221e1122e1111e",
)


def decay(coef):
    root = (-1.0 + np.sqrt(1.0 - 4.0 * coef * coef)) / (2.0 * coef)
    return float(root), float(1.0 / (1.0 + 2.0 * coef * root))


ROOTS = tuple(decay(coef)[0] for coef in COEFS)


def inner_weights(system):
    root, gain = decay(COEFS[system])
    return (gain, gain / root, gain * root), (gain, gain * root, gain * root)


def wall_weights(system):
    root, gain = decay(COEFS[system])
    size = 96
    band = np.full(size, COEFS[system])
    band[0], band[1] = 0.0, WALL_COEFS[system]
    matrix = np.eye(size) + np.diag(band[:-1], 1) + np.diag(band[1:], -1)
    inverse = np.linalg.solve(matrix, np.eye(size)[:, :3])
    spread = (inverse[:2, 2] - gain * root ** np.abs(np.arange(2) - 2.0)) / root**2
    columns = np.stack([inverse[:2, 0], inverse[:2, 1], spread], axis=1)
    return tuple(map(float, columns[1] / root)), tuple(map(float, columns[0]))


def iota(shape, axis):
    return lax.broadcasted_iota(jnp.int32, shape, axis)


def powers(root, exponent):
    size = jnp.exp(exponent.astype(jnp.float32) * float(np.log(-root)))
    return jnp.where(lax.rem(exponent, 2) == 0, size, -size)


def stencils(minus_two, minus_one, centre, plus_one, plus_two):
    first = 7.0 / 9.0 * (plus_one - minus_one) + 1.0 / 36.0 * (plus_two - minus_two)
    second = 12.0 / 11.0 * (plus_one - 2.0 * centre + minus_one) + 3.0 / 44.0 * (
        plus_two - 2.0 * centre + minus_two
    )
    return first, second


def right_sides(lines):
    turn = lambda steps: pltpu.roll(lines, steps % lines.shape[0], 0)
    at = iota(lines.shape, 0)
    inner = (at >= 2) & (at < lines.shape[0] - 2)
    parts = stencils(turn(2), turn(1), lines, turn(-1), turn(-2))
    return [jnp.where(inner, part, 0.0) for part in parts]


def ramps(lanes):
    at = iota((TILE, lanes), 0)
    return [(powers(root, at), powers(root, TILE - 1 - at)) for root in ROOTS]


def difference_sums(lines, ramp):
    rows, lanes = lines.shape
    steps = pltpu.roll(lines, rows - 1, 0) - lines
    tiles = [steps[k : k + TILE] for k in range(0, rows, TILE)]
    tiles[-1] = jnp.where(iota((TILE, lanes), 0) == TILE - 1, 0.0, tiles[-1])
    sums = []
    for root, (up, down) in zip(ROOTS, ramp):
        step = float(root**TILE)
        low, high = tiles[-1], tiles[0]
        for tile in tiles[-2::-1]:
            low = low * step + tile
        for tile in tiles[1:]:
            high = high * step + tile
        sums.append(jnp.sum(low * up, axis=0, keepdims=True))
        sums.append(jnp.sum(high * down, axis=0, keepdims=True))
    return sums


def right_side_sums(layers, sums, rows):
    (one, two), size = ROOTS, rows
    steps = [[line[k + 1] - line[k] for k in range(3)] for line in layers]
    bends = [[line[k + 1] - line[k] for k in range(2)] for line in steps]
    near, far = 7.0 / 9.0 + 1.0 / 36.0, 1.0 / 36.0
    mid, side = 12.0 / 11.0 + 6.0 / 44.0, 3.0 / 44.0
    result = []
    for end in range(2):
        d0, d1, d2 = steps[end]
        z0, z1, z2 = [-step for step in steps[1 - end]]
        e1, e2 = bends[end]
        y1, y2 = bends[1 - end]
        total = sums[0] if end == 0 else sums[1] * float(-1.0 / one)
        last0, last1, last2 = [z * float(one ** (size - 2 - k)) for k, z in enumerate((z0, z1, z2))]
        first = (
            near * (total - d0 - one * d1 - last0)
            + (near * one) * (total - d0 - last0 - last1)
            + (far / one) * (total - d0 - one * d1 - one * one * d2)
            + (far * one * one) * (total - last0 - last1 - last2)
        )
        total = sums[2] if end == 0 else sums[3] * float(-1.0 / two)
        total = (1.0 - two) * total - d0 + z0 * float(two ** (size - 1))
        last1, last2 = y1 * float(two ** (size - 2)), y2 * float(two ** (size - 3))
        second = (
            mid * (total - two * e1 - last1)
            + (side / two) * (total - two * e1 - two * two * e2)
            + (side * two) * (total - last1 - last2)
        )
        result.append((first if end == 0 else -first, second))
    return result


def sent_rows(layers, sums, sign):
    b1, b2, b3, b4 = layers
    d2, d3, d4 = b2 - b1, b3 - b1, b4 - b1
    one, two = ROOTS
    first = 7.0 / 9.0 * (d2 + one * d3) + 1.0 / 36.0 * (d3 + one * d4)
    second = 12.0 / 11.0 * (d2 + two * (d3 - 2.0 * d2)) + 3.0 / 44.0 * (d3 + two * (d4 - 2.0 * d2))
    return [b1, b2, sums[0] - sign * first, sums[1] + second]


def turned(field):
    slabs, rows, lanes = field.shape
    fill = -(slabs * rows) % lanes
    lines = field.reshape(slabs * rows, lanes)
    if fill:
        lines = jnp.concatenate([lines, jnp.zeros((fill, lanes), jnp.float32)], axis=0)
    return jnp.transpose(lines)


def kind_of(x, y):
    return 8 * (x % 2) + 4 * (x // 2 % 2) + 2 * (y % 2) + y // 2 % 2


def beyond(way, kind):
    return kind ^ {"e": 8, "o": 12, "1": 2, "2": 3}[way]


def arrival_rounds(way):
    return [
        next(k for k, ways in enumerate(ROUNDS) if ways[beyond(way, kind)] == way)
        for kind in range(16)
    ]


def by_kind(numbers, options):
    packed = np.int64(sum(number << 2 * kind for kind, number in enumerate(numbers)))
    kind = kind_of(lax.axis_index("gx"), lax.axis_index("gy"))
    number = lax.shift_right_logical(jnp.int32(packed.astype(np.int32)), 2 * kind) & 3
    first, *others = sorted(set(numbers))
    chosen = options[first]
    for other in others:
        chosen = jnp.where(number == other, options[other], chosen)
    return chosen


def ends_of(groups, ramp):
    rows = groups[0].shape[0]
    stack = lambda values: jnp.concatenate(values, axis=0)
    layers = [
        [stack([group[at : at + 1] for group in groups]) for at in range(4)],
        [stack([group[rows - 1 - at : rows - at] for group in groups]) for at in range(4)],
    ]
    sums = [stack(values) for values in zip(*[difference_sums(group, ramp) for group in groups])]
    return layers, right_side_sums(layers, sums, rows)


def sends(layers, sums, even):
    low = sent_rows(layers[0], sums[0], -1.0)
    high = sent_rows(layers[1], sums[1], 1.0)
    return select(even, high, low), select(even, low, high)


def send_kernel(field, stretch, metric, _, *refs):
    *outs, metrics, x_own, y_own = refs
    metrics[...] = metric_rows(stretch, metric)
    slabs, _, lanes = field.shape
    x_even = lax.rem(lax.axis_index("gx"), 2) == 0
    y_even = lax.rem(lax.axis_index("gy"), 2) == 0
    groups = [field[s] for s in range(slabs)]
    ramp = ramps(lanes)
    layers, sums = ends_of(groups, ramp)
    sent = dict(zip("eo", sends(layers, sums, x_even)))
    for k, layer in enumerate(layers[0] + layers[1]):
        x_own[k, :slabs] = layer
    lines = turned(field[...])
    layers, sums = ends_of(
        [lines[:, k : k + lanes] for k in range(0, lines.shape[1], lanes)], ramp
    )
    sent.update(zip("12", sends(layers, sums, y_even)))
    for k, values in enumerate([*layers[0], *sums[0], *layers[1], *sums[1]]):
        y_own[k, : values.shape[0]] = values
    for out, ways in zip(outs, ROUNDS):
        count = out.shape[0] // 4
        options = {}
        for number, way in enumerate(WAYS):
            if way in ways:
                fill = jnp.zeros((count - sent[way][0].shape[0], lanes), jnp.float32)
                parts = [part for value in sent[way] for part in (value, fill) if part.shape[0]]
                options[number] = jnp.concatenate(parts, axis=0)
        out[...] = by_kind([WAYS.index(way) for way in ways], options)


def inverse_matrix(system, size):
    root, gain = decay(COEFS[system])
    return gain * powers(root, jnp.abs(iota((size, size), 0) - iota((size, size), 1)))


def solve(matrix, right_side):
    return jnp.dot(matrix, right_side, precision=HIGHEST, preferred_element_type=jnp.float32)


def table_kernel(y_out, x_out):
    for system in range(2):
        y_out[system] = inverse_matrix(system, y_out.shape[1])
        x_out[system] = inverse_matrix(system, x_out.shape[1])


def metric_rows(stretch, metric):
    position = pl.ds(lax.axis_index("gy"), 1)
    inv = 1.0 / stretch[position, :]
    curve = VISCOSITY * metric[position, :] * inv * inv * inv
    fill = jnp.zeros((TILE - 3, inv.shape[1]), jnp.float32)
    return jnp.concatenate([inv, curve, VISCOSITY * inv * inv, fill], axis=0)


def bulk_kernel(
    field, metrics, x_own, y_own, y_matrix, x_matrix,
    out, slope_turned, bend_turned, x_shares, y_shares,
):
    slabs, rows, lanes = field.shape
    y_at, y_count = lax.axis_index("gy"), lax.axis_size("gy")
    own = [x_own[k] for k in range(8)]
    shares = own_numbers(own[:4], 1.0) + own_numbers(own[4:], -1.0)
    for k, share in enumerate(shares):
        x_shares[k] = share
    own = [y_own[k] for k in range(12)]
    shares = own_numbers(own[:4], 1.0, y_at == 0, own[4:6])
    shares += own_numbers(own[6:10], -1.0, y_at == y_count - 1, own[10:])
    for k, share in enumerate(shares):
        y_shares[k] = share
    inv, curve, bend = metrics[0:1, :], metrics[1:2, :], metrics[2:3, :]
    bend = jnp.transpose(jnp.broadcast_to(bend, (lanes, lanes)))
    bend_turned[...] = bend
    slope = [-(field[plane * 3 + 1] * inv + curve) for plane in range(slabs // 3)]
    slope = turned(jnp.stack([part for part in slope for _ in range(3)], axis=0))
    slope_turned[...] = slope
    first, second = right_sides(turned(field[...]))
    y_term = slope * solve(y_matrix[0], first) + bend[:, :1] * solve(y_matrix[1], second)
    y_term = jnp.transpose(y_term)
    for s in range(slabs):
        first, second = right_sides(field[s])
        x_term = VISCOSITY * solve(x_matrix[1], second) - field[s // 3 * 3] * solve(x_matrix[0], first)
        out[s] = x_term + y_term[s * rows : (s + 1) * rows]


def weigh(weights, values):
    return weights[0] * values[0] + weights[1] * values[1] + weights[2] * values[2]


def own_numbers(own, sign, wall=None, sums=None):
    a2, a3, a4 = [layer - own[0] for layer in own[1:]]
    first = (
        sign * (7.0 / 9.0 * a2 + 1.0 / 36.0 * a3),
        sign * (7.0 / 9.0 * a3 + 1.0 / 36.0 * a4),
        sign * (1.0 / 36.0 * a2),
    )
    second = (
        12.0 / 11.0 * a2 + 3.0 / 44.0 * a3,
        12.0 / 11.0 * (a3 - 2.0 * a2) + 3.0 / 44.0 * (a4 - 2.0 * a2),
        3.0 / 44.0 * a2,
    )
    numbers = []
    for system, rows in enumerate((first, second)):
        numbers += [weigh(weights, rows) for weights in inner_weights(system)]
    if wall is None:
        return numbers
    first = (sign * (2.0 * a2 - 0.5 * a3), sign * 0.75 * a3, sums[0])
    second = (4.0 * a3 - 5.0 * a2 - a4, 1.2 * (a3 - 2.0 * a2), sums[1])
    at_wall = []
    for system, rows in enumerate((first, second)):
        at_wall += [weigh(weights, rows) for weights in wall_weights(system)]
    return [jnp.where(wall, there, here) for there, here in zip(at_wall, numbers)]


def edge_numbers(shares, nearest, received, sign, wall=None):
    b1, b2 = received[0] - nearest, received[1] - nearest
    numbers = []
    for system, root in enumerate(ROOTS):
        pair = []
        for share, (w0, w1, w2) in zip(shares[2 * system :], inner_weights(system)):
            if system == 0:
                near = -sign * (7.0 / 9.0 * (w0 + w2) + 1.0 / 36.0 * (w1 + w2 * (1.0 + root)))
                next_one = -sign * (1.0 / 36.0 * w0)
            else:
                near = 12.0 / 11.0 * (w0 - w2) + 3.0 / 44.0 * (w1 - w2 * (1.0 + root))
                next_one = 3.0 / 44.0 * w0
            part = near * b1 + next_one * b2 + w2 * received[2 + system]
            pair.append(share + (part if wall is None else jnp.where(wall, 0.0, part)))
        numbers.append(pair)
    return numbers


def edge_tiles(numbers, line, side, ramp):
    tiles = []
    for (spread, first), powers_of in zip(numbers, ramp):
        far = powers_of[side] * spread[line : line + 1]
        at_edge = iota(far.shape, 0) == (TILE - 1 if side else 0)
        tiles.append((jnp.where(at_edge, first[line : line + 1], far), far))
    return tiles


def received(way, moved, groups):
    rounds = arrival_rounds(way)
    numbers = []
    for k in range(4):
        values = {
            at: moved[at][pl.ds(k * (moved[at].shape[0] // 4), groups), :] for at in set(rounds)
        }
        numbers.append(by_kind(rounds, values))
    return numbers


def select(flag, one, two):
    return [jnp.where(flag, there, here) for there, here in zip(one, two)]


def edge_update(low, high, root, tile, tiles):
    parts = []
    for (near, far), steps in ((low, tile), (high, tiles - 1 - tile)):
        scale = float(root ** (TILE * steps))
        if abs(scale) > np.finfo(np.float32).tiny:
            parts.append(far * scale if steps else near)
    return sum(parts[1:], parts[0]) if parts else None


def final_kernel(
    field, bulk, slope, bend, x_shares, y_shares, x_own, y_own, *refs
):
    *moved, out = refs
    slabs, rows, lanes = field.shape
    y_at, y_count = lax.axis_index("gy"), lax.axis_size("gy")
    x_even = lax.rem(lax.axis_index("gx"), 2) == 0
    y_even = lax.rem(y_at, 2) == 0
    groups = slope.shape[1] // lanes
    shares = [y_shares[k, :groups] for k in range(8)]
    even, odd = [received(way, moved, groups) for way in "12"]
    from_low, from_high = select(y_even, odd, even), select(y_even, even, odd)
    low = edge_numbers(shares[:4], y_own[0, :groups], from_low, 1.0, y_at == 0)
    high = edge_numbers(shares[4:], y_own[6, :groups], from_high, -1.0, y_at == y_count - 1)
    tiles, ramp = lanes // TILE, ramps(lanes)
    y_term = []
    for group in range(groups):
        at_low, at_high = edge_tiles(low, group, 0, ramp), edge_tiles(high, group, 1, ramp)
        part = slice(group * lanes, (group + 1) * lanes)
        column = []
        for tile in range(tiles):
            place = slice(tile * TILE, (tile + 1) * TILE)
            one, two = [edge_update(at_low[k], at_high[k], ROOTS[k], tile, tiles) for k in range(2)]
            term = slope[place, part] * one
            column.append(term if two is None else term + bend[place, :] * two)
        y_term.append(jnp.transpose(jnp.concatenate(column, axis=0)))
    y_term = jnp.concatenate(y_term, axis=0)
    shares = [x_shares[k, :slabs] for k in range(8)]
    even, odd = [received(way, moved, slabs) for way in "eo"]
    low = edge_numbers(shares[:4], x_own[0, :slabs], select(x_even, odd, even), 1.0)
    high = edge_numbers(shares[4:], x_own[4, :slabs], select(x_even, even, odd), -1.0)
    for _, second in (low, high):
        second[:] = [VISCOSITY * number for number in second]
    tiles = rows // TILE
    for s in range(slabs):
        at_low, at_high = edge_tiles(low, s, 0, ramp), edge_tiles(high, s, 1, ramp)
        for tile in range(tiles):
            place = slice(tile * TILE, (tile + 1) * TILE)
            one, two = [edge_update(at_low[k], at_high[k], ROOTS[k], tile, tiles) for k in range(2)]
            turned = y_term[s * rows + tile * TILE : s * rows + (tile + 1) * TILE]
            x_term = two - field[s // 3 * 3, place] * one
            out[s, place] = bulk[s, place] + x_term + turned


def partner(way, x, y, x_count, y_count):
    if way == "2" and y in (0, y_count - 1):
        way = "e"
    if way in "eo":
        step = 1 if (x % 2 == 0) == (way == "e") else -1
        return (x + step) % x_count, y
    return x, y + (1 if (y % 2 == 0) == (way == "1") else -1)


def exchange_pairs(ways, x_count, y_count):
    at = lambda x, y: x * y_count + y
    return [
        (at(x, y), at(*partner(ways[kind_of(x, y)], x, y, x_count, y_count)))
        for x in range(x_count)
        for y in range(y_count)
    ]


def call(kernel, outs, name, flops, out_space=pltpu.VMEM, scratch=()):
    return lambda *args: pl.pallas_call(
        kernel,
        out_shape=outs,
        in_specs=[pl.BlockSpec(memory_space=pltpu.VMEM)] * len(args),
        out_specs=[pl.BlockSpec(memory_space=out_space)] * len(outs),
        scratch_shapes=scratch,
        cost_estimate=pl.CostEstimate(flops=flops, bytes_accessed=0, transcendentals=0),
        compiler_params=pltpu.CompilerParams(vmem_limit_bytes=8 * 2**20),
        name=name,
    )(*args)


def shards(velocity, stretch, second_metric):
    planes, comps, rows, lanes = velocity.shape
    slabs = planes * comps
    x_count, y_count = lax.axis_size("gx"), lax.axis_size("gy")
    stretch = stretch.reshape(y_count, lanes)
    metric = second_metric.reshape(y_count, lanes)
    shape = lambda *dims: jax.ShapeDtypeStruct(dims, jnp.float32)
    block = shape(slabs, rows, lanes)
    move = lambda value, ways: lax.ppermute(
        value, ("gx", "gy"), exchange_pairs(ways, x_count, y_count)
    )

    tables = call(table_kernel, [shape(2, lanes, lanes), shape(2, rows, rows)], "tables", 10**8)()
    field = velocity.reshape(slabs, rows, lanes)
    groups = -(-slabs * rows // lanes)
    send = shape(4 * max(slabs, groups), lanes)
    *sent, metrics, x_own, y_own = call(
        send_kernel,
        [send] * len(ROUNDS)
        + [shape(TILE, lanes), shape(8, TILE, lanes), shape(12, TILE, lanes)],
        "sends",
        10**6,
    )(field, stretch, metric, tables[1])
    moved = [move(value, ways) for value, ways in zip(sent, ROUNDS)]
    bulk = call(
        bulk_kernel,
        [block, shape(lanes, groups * lanes), shape(lanes, lanes)] + [shape(8, TILE, lanes)] * 2,
        "bulk",
        10**8,
    )(field, metrics, x_own, y_own, *tables)
    (out,) = call(
        final_kernel,
        [block],
        "final",
        10**7,
    )(field, *bulk, x_own, y_own, *moved)
    return out.reshape(planes, comps, rows, lanes)


def solution(mesh):
    return jax.shard_map(
        shards,
        mesh=mesh,
        in_specs=(P(None, None, "gx", "gy"), P(), P()),
        out_specs=P(None, None, "gx", "gy"),
        check_vma=False,
    )
```

```python
import jax
import jax.numpy as jnp
import numpy as np
from jax import lax
from jax.experimental import pallas as pl
from jax.experimental.pallas import tpu as pltpu
from jax.sharding import PartitionSpec as P

VISCOSITY = 0.5
COEFS = (1.0 / 3.0, 2.0 / 11.0)
WALL_COEFS = (1.0 / 4.0, 1.0 / 10.0)
HIGHEST = lax.Precision.HIGHEST
TILE = 8
WAYS = "eo12"
ROUNDS = (
    "2oeo22eooe22oeo2",
    "o211oo2e11ooe22o",
    "1eoee1o2eo1e2oe1",
    "e1221e1122e1111e",
)


def decay(coef):
    root = (-1.0 + np.sqrt(1.0 - 4.0 * coef * coef)) / (2.0 * coef)
    return float(root), float(1.0 / (1.0 + 2.0 * coef * root))


ROOTS = tuple(decay(coef)[0] for coef in COEFS)


def inner_weights(system):
    root, gain = decay(COEFS[system])
    return (gain, gain / root, gain * root), (gain, gain * root, gain * root)


def wall_weights(system):
    root, gain = decay(COEFS[system])
    size = 96
    band = np.full(size, COEFS[system])
    band[0], band[1] = 0.0, WALL_COEFS[system]
    matrix = np.eye(size) + np.diag(band[:-1], 1) + np.diag(band[1:], -1)
    inverse = np.linalg.solve(matrix, np.eye(size)[:, :3])
    spread = (inverse[:2, 2] - gain * root ** np.abs(np.arange(2) - 2.0)) / root**2
    columns = np.stack([inverse[:2, 0], inverse[:2, 1], spread], axis=1)
    return tuple(map(float, columns[1] / root)), tuple(map(float, columns[0]))


def iota(shape, axis):
    return lax.broadcasted_iota(jnp.int32, shape, axis)


def powers(root, exponent):
    size = jnp.exp(exponent.astype(jnp.float32) * float(np.log(-root)))
    return jnp.where(lax.rem(exponent, 2) == 0, size, -size)


def stencils(minus_two, minus_one, centre, plus_one, plus_two):
    first = 7.0 / 9.0 * (plus_one - minus_one) + 1.0 / 36.0 * (plus_two - minus_two)
    second = 12.0 / 11.0 * (plus_one - 2.0 * centre + minus_one) + 3.0 / 44.0 * (
        plus_two - 2.0 * centre + minus_two
    )
    return first, second


def right_sides(lines):
    turn = lambda steps: pltpu.roll(lines, steps % lines.shape[0], 0)
    at = iota(lines.shape, 0)
    inner = (at >= 2) & (at < lines.shape[0] - 2)
    parts = stencils(turn(2), turn(1), lines, turn(-1), turn(-2))
    return [jnp.where(inner, part, 0.0) for part in parts]


def ramps(lanes):
    at = iota((TILE, lanes), 0)
    return [(powers(root, at), powers(root, TILE - 1 - at)) for root in ROOTS]


def difference_sums(lines, ramp):
    rows, lanes = lines.shape
    steps = pltpu.roll(lines, rows - 1, 0) - lines
    tiles = [steps[k : k + TILE] for k in range(0, rows, TILE)]
    tiles[-1] = jnp.where(iota((TILE, lanes), 0) == TILE - 1, 0.0, tiles[-1])
    sums = []
    for root, (up, down) in zip(ROOTS, ramp):
        step = float(root**TILE)
        reach = sum(16.0 * abs(step) ** k > np.finfo(np.float32).tiny for k in range(len(tiles)))
        near_low, near_high = tiles[:reach], tiles[len(tiles) - reach :]
        low, high = near_low[-1], near_high[0]
        for tile in near_low[-2::-1]:
            low = low * step + tile
        for tile in near_high[1:]:
            high = high * step + tile
        sums.append(jnp.sum(low * up, axis=0, keepdims=True))
        sums.append(jnp.sum(high * down, axis=0, keepdims=True))
    return sums


def right_side_sums(layers, sums, rows):
    (one, two), size = ROOTS, rows
    steps = [[line[k + 1] - line[k] for k in range(3)] for line in layers]
    bends = [[line[k + 1] - line[k] for k in range(2)] for line in steps]
    near, far = 7.0 / 9.0 + 1.0 / 36.0, 1.0 / 36.0
    mid, side = 12.0 / 11.0 + 6.0 / 44.0, 3.0 / 44.0
    result = []
    for end in range(2):
        d0, d1, d2 = steps[end]
        z0, z1, z2 = [-step for step in steps[1 - end]]
        e1, e2 = bends[end]
        y1, y2 = bends[1 - end]
        total = sums[0] if end == 0 else sums[1] * float(-1.0 / one)
        last0, last1, last2 = [z * float(one ** (size - 2 - k)) for k, z in enumerate((z0, z1, z2))]
        first = (
            near * (total - d0 - one * d1 - last0)
            + (near * one) * (total - d0 - last0 - last1)
            + (far / one) * (total - d0 - one * d1 - one * one * d2)
            + (far * one * one) * (total - last0 - last1 - last2)
        )
        total = sums[2] if end == 0 else sums[3] * float(-1.0 / two)
        total = (1.0 - two) * total - d0 + z0 * float(two ** (size - 1))
        last1, last2 = y1 * float(two ** (size - 2)), y2 * float(two ** (size - 3))
        second = (
            mid * (total - two * e1 - last1)
            + (side / two) * (total - two * e1 - two * two * e2)
            + (side * two) * (total - last1 - last2)
        )
        result.append((first if end == 0 else -first, second))
    return result


def sent_rows(layers, sums, sign):
    b1, b2, b3, b4 = layers
    d2, d3, d4 = b2 - b1, b3 - b1, b4 - b1
    one, two = ROOTS
    first = 7.0 / 9.0 * (d2 + one * d3) + 1.0 / 36.0 * (d3 + one * d4)
    second = 12.0 / 11.0 * (d2 + two * (d3 - 2.0 * d2)) + 3.0 / 44.0 * (d3 + two * (d4 - 2.0 * d2))
    return [b1, b2, sums[0] - sign * first, sums[1] + second]


def turned(field):
    slabs, rows, lanes = field.shape
    fill = -(slabs * rows) % lanes
    lines = field.reshape(slabs * rows, lanes)
    if fill:
        lines = jnp.concatenate([lines, jnp.zeros((fill, lanes), jnp.float32)], axis=0)
    return jnp.transpose(lines)


def kind_of(x, y):
    return 8 * (x % 2) + 4 * (x // 2 % 2) + 2 * (y % 2) + y // 2 % 2


def beyond(way, kind):
    return kind ^ {"e": 8, "o": 12, "1": 2, "2": 3}[way]


def arrival_rounds(way):
    return [
        next(k for k, ways in enumerate(ROUNDS) if ways[beyond(way, kind)] == way)
        for kind in range(16)
    ]


def by_kind(numbers, options):
    packed = np.int64(sum(number << 2 * kind for kind, number in enumerate(numbers)))
    kind = kind_of(lax.axis_index("gx"), lax.axis_index("gy"))
    number = lax.shift_right_logical(jnp.int32(packed.astype(np.int32)), 2 * kind) & 3
    first, *others = sorted(set(numbers))
    chosen = options[first]
    for other in others:
        chosen = jnp.where(number == other, options[other], chosen)
    return chosen


def ends_of(groups, ramp):
    rows = groups[0].shape[0]
    stack = lambda values: jnp.concatenate(values, axis=0)
    layers = [
        [stack([group[at : at + 1] for group in groups]) for at in range(4)],
        [stack([group[rows - 1 - at : rows - at] for group in groups]) for at in range(4)],
    ]
    sums = [stack(values) for values in zip(*[difference_sums(group, ramp) for group in groups])]
    return layers, right_side_sums(layers, sums, rows)


def sends(layers, sums, even):
    low = sent_rows(layers[0], sums[0], -1.0)
    high = sent_rows(layers[1], sums[1], 1.0)
    return select(even, high, low), select(even, low, high)


def send_kernel(field, stretch, metric, _, *refs):
    *outs, metrics, x_own, y_own = refs
    metrics[...] = metric_rows(stretch, metric)
    slabs, _, lanes = field.shape
    x_even = lax.rem(lax.axis_index("gx"), 2) == 0
    y_even = lax.rem(lax.axis_index("gy"), 2) == 0
    groups = [field[s] for s in range(slabs)]
    ramp = ramps(lanes)
    layers, sums = ends_of(groups, ramp)
    sent = dict(zip("eo", sends(layers, sums, x_even)))
    for k, layer in enumerate(layers[0] + layers[1]):
        x_own[k, :slabs] = layer
    lines = turned(field[...])
    layers, sums = ends_of(
        [lines[:, k : k + lanes] for k in range(0, lines.shape[1], lanes)], ramp
    )
    sent.update(zip("12", sends(layers, sums, y_even)))
    for k, values in enumerate([*layers[0], *sums[0], *layers[1], *sums[1]]):
        y_own[k, : values.shape[0]] = values
    count = outs[0].shape[0] // 4
    packed = []
    for way in WAYS:
        fill = jnp.zeros((count - sent[way][0].shape[0], lanes), jnp.float32)
        parts = [part for value in sent[way] for part in (value, fill) if part.shape[0]]
        packed.append(jnp.concatenate(parts, axis=0))
    for out, ways in zip(outs, ROUNDS):
        out[...] = by_kind([WAYS.index(way) for way in ways], packed)


def inverse_matrix(system, size):
    root, gain = decay(COEFS[system])
    return gain * powers(root, jnp.abs(iota((size, size), 0) - iota((size, size), 1)))


def solve(matrix, right_side):
    return jnp.dot(matrix, right_side, precision=HIGHEST, preferred_element_type=jnp.float32)


def table_kernel(y_out, x_out):
    for system in range(2):
        y_out[system] = inverse_matrix(system, y_out.shape[1])
        x_out[system] = inverse_matrix(system, x_out.shape[1])


def metric_rows(stretch, metric):
    position = pl.ds(lax.axis_index("gy"), 1)
    inv = 1.0 / stretch[position, :]
    curve = VISCOSITY * metric[position, :] * inv * inv * inv
    fill = jnp.zeros((TILE - 3, inv.shape[1]), jnp.float32)
    return jnp.concatenate([inv, curve, VISCOSITY * inv * inv, fill], axis=0)


def bulk_kernel(
    field, metrics, x_own, y_own, y_matrix, x_matrix,
    out, slope_turned, bend_turned, x_shares, y_shares,
):
    slabs, rows, lanes = field.shape
    y_at, y_count = lax.axis_index("gy"), lax.axis_size("gy")
    own = [x_own[k] for k in range(8)]
    shares = own_numbers(own[:4], 1.0) + own_numbers(own[4:], -1.0)
    for k, share in enumerate(shares):
        x_shares[k] = share
    own = [y_own[k] for k in range(12)]
    shares = own_numbers(own[:4], 1.0, y_at == 0, own[4:6])
    shares += own_numbers(own[6:10], -1.0, y_at == y_count - 1, own[10:])
    for k, share in enumerate(shares):
        y_shares[k] = share
    inv, curve, bend = metrics[0:1, :], metrics[1:2, :], metrics[2:3, :]
    bend = jnp.transpose(jnp.broadcast_to(bend, (lanes, lanes)))
    bend_turned[...] = bend
    slope = [-(field[plane * 3 + 1] * inv + curve) for plane in range(slabs // 3)]
    slope = turned(jnp.stack([part for part in slope for _ in range(3)], axis=0))
    slope_turned[...] = slope
    first, second = right_sides(turned(field[...]))
    y_term = slope * solve(y_matrix[0], first) + bend[:, :1] * solve(y_matrix[1], second)
    y_term = jnp.transpose(y_term)
    for s in range(slabs):
        first, second = right_sides(field[s])
        x_term = VISCOSITY * solve(x_matrix[1], second) - field[s // 3 * 3] * solve(x_matrix[0], first)
        out[s] = x_term + y_term[s * rows : (s + 1) * rows]


def weigh(weights, values):
    return weights[0] * values[0] + weights[1] * values[1] + weights[2] * values[2]


def own_numbers(own, sign, wall=None, sums=None):
    a2, a3, a4 = [layer - own[0] for layer in own[1:]]
    first = (
        sign * (7.0 / 9.0 * a2 + 1.0 / 36.0 * a3),
        sign * (7.0 / 9.0 * a3 + 1.0 / 36.0 * a4),
        sign * (1.0 / 36.0 * a2),
    )
    second = (
        12.0 / 11.0 * a2 + 3.0 / 44.0 * a3,
        12.0 / 11.0 * (a3 - 2.0 * a2) + 3.0 / 44.0 * (a4 - 2.0 * a2),
        3.0 / 44.0 * a2,
    )
    numbers = []
    for system, rows in enumerate((first, second)):
        numbers += [weigh(weights, rows) for weights in inner_weights(system)]
    if wall is None:
        return numbers
    first = (sign * (2.0 * a2 - 0.5 * a3), sign * 0.75 * a3, sums[0])
    second = (4.0 * a3 - 5.0 * a2 - a4, 1.2 * (a3 - 2.0 * a2), sums[1])
    at_wall = []
    for system, rows in enumerate((first, second)):
        at_wall += [weigh(weights, rows) for weights in wall_weights(system)]
    return [jnp.where(wall, there, here) for there, here in zip(at_wall, numbers)]


def edge_numbers(shares, nearest, received, sign, wall=None):
    b1, b2 = received[0] - nearest, received[1] - nearest
    numbers = []
    for system, root in enumerate(ROOTS):
        pair = []
        for share, (w0, w1, w2) in zip(shares[2 * system :], inner_weights(system)):
            if system == 0:
                near = -sign * (7.0 / 9.0 * (w0 + w2) + 1.0 / 36.0 * (w1 + w2 * (1.0 + root)))
                next_one = -sign * (1.0 / 36.0 * w0)
            else:
                near = 12.0 / 11.0 * (w0 - w2) + 3.0 / 44.0 * (w1 - w2 * (1.0 + root))
                next_one = 3.0 / 44.0 * w0
            part = near * b1 + next_one * b2 + w2 * received[2 + system]
            pair.append(share + (part if wall is None else jnp.where(wall, 0.0, part)))
        numbers.append(pair)
    return numbers


def edge_tiles(numbers, line, side, ramp):
    tiles = []
    for (spread, first), powers_of in zip(numbers, ramp):
        far = powers_of[side] * spread[line : line + 1]
        at_edge = iota(far.shape, 0) == (TILE - 1 if side else 0)
        tiles.append((jnp.where(at_edge, first[line : line + 1], far), far))
    return tiles


def received(way, moved, groups):
    packed = by_kind(arrival_rounds(way), [part[...] for part in moved])
    count = packed.shape[0] // 4
    return [packed[k * count : k * count + groups] for k in range(4)]


def select(flag, one, two):
    return [jnp.where(flag, there, here) for there, here in zip(one, two)]


def edge_update(low, high, root, tile, tiles):
    parts = []
    for (near, far), steps in ((low, tile), (high, tiles - 1 - tile)):
        scale = float(root ** (TILE * steps))
        if abs(scale) > np.finfo(np.float32).tiny:
            parts.append(far * scale if steps else near)
    return sum(parts[1:], parts[0]) if parts else None


def final_kernel(
    field, bulk, slope, bend, x_shares, y_shares, x_own, y_own, *refs
):
    *moved, out = refs
    slabs, rows, lanes = field.shape
    y_at, y_count = lax.axis_index("gy"), lax.axis_size("gy")
    x_even = lax.rem(lax.axis_index("gx"), 2) == 0
    y_even = lax.rem(y_at, 2) == 0
    groups = slope.shape[1] // lanes
    shares = [y_shares[k, :groups] for k in range(8)]
    even, odd = [received(way, moved, groups) for way in "12"]
    from_low, from_high = select(y_even, odd, even), select(y_even, even, odd)
    low = edge_numbers(shares[:4], y_own[0, :groups], from_low, 1.0, y_at == 0)
    high = edge_numbers(shares[4:], y_own[6, :groups], from_high, -1.0, y_at == y_count - 1)
    tiles, ramp = lanes // TILE, ramps(lanes)
    y_term = []
    for group in range(groups):
        at_low, at_high = edge_tiles(low, group, 0, ramp), edge_tiles(high, group, 1, ramp)
        part = slice(group * lanes, (group + 1) * lanes)
        column = []
        for tile in range(tiles):
            place = slice(tile * TILE, (tile + 1) * TILE)
            one, two = [edge_update(at_low[k], at_high[k], ROOTS[k], tile, tiles) for k in range(2)]
            term = slope[place, part] * one
            column.append(term if two is None else term + bend[place, :] * two)
        y_term.append(jnp.transpose(jnp.concatenate(column, axis=0)))
    y_term = jnp.concatenate(y_term, axis=0)
    shares = [x_shares[k, :slabs] for k in range(8)]
    even, odd = [received(way, moved, slabs) for way in "eo"]
    low = edge_numbers(shares[:4], x_own[0, :slabs], select(x_even, odd, even), 1.0)
    high = edge_numbers(shares[4:], x_own[4, :slabs], select(x_even, even, odd), -1.0)
    for _, second in (low, high):
        second[:] = [VISCOSITY * number for number in second]
    tiles = rows // TILE
    for s in range(slabs):
        at_low, at_high = edge_tiles(low, s, 0, ramp), edge_tiles(high, s, 1, ramp)
        for tile in range(tiles):
            place = slice(tile * TILE, (tile + 1) * TILE)
            one, two = [edge_update(at_low[k], at_high[k], ROOTS[k], tile, tiles) for k in range(2)]
            turned = y_term[s * rows + tile * TILE : s * rows + (tile + 1) * TILE]
            x_term = two - field[s // 3 * 3, place] * one
            out[s, place] = bulk[s, place] + x_term + turned


def partner(way, x, y, x_count, y_count):
    if way == "2" and y in (0, y_count - 1):
        way = "e"
    if way in "eo":
        step = 1 if (x % 2 == 0) == (way == "e") else -1
        return (x + step) % x_count, y
    return x, y + (1 if (y % 2 == 0) == (way == "1") else -1)


def exchange_pairs(ways, x_count, y_count):
    at = lambda x, y: x * y_count + y
    return [
        (at(x, y), at(*partner(ways[kind_of(x, y)], x, y, x_count, y_count)))
        for x in range(x_count)
        for y in range(y_count)
    ]


def call(kernel, outs, name, flops, out_space=pltpu.VMEM, scratch=()):
    return lambda *args: pl.pallas_call(
        kernel,
        out_shape=outs,
        in_specs=[pl.BlockSpec(memory_space=pltpu.VMEM)] * len(args),
        out_specs=[pl.BlockSpec(memory_space=out_space)] * len(outs),
        scratch_shapes=scratch,
        cost_estimate=pl.CostEstimate(flops=flops, bytes_accessed=0, transcendentals=0),
        compiler_params=pltpu.CompilerParams(vmem_limit_bytes=8 * 2**20),
        name=name,
    )(*args)


def shards(velocity, stretch, second_metric):
    planes, comps, rows, lanes = velocity.shape
    slabs = planes * comps
    x_count, y_count = lax.axis_size("gx"), lax.axis_size("gy")
    stretch = stretch.reshape(y_count, lanes)
    metric = second_metric.reshape(y_count, lanes)
    shape = lambda *dims: jax.ShapeDtypeStruct(dims, jnp.float32)
    block = shape(slabs, rows, lanes)
    move = lambda value, ways: lax.ppermute(
        value, ("gx", "gy"), exchange_pairs(ways, x_count, y_count)
    )

    tables = call(table_kernel, [shape(2, lanes, lanes), shape(2, rows, rows)], "tables", 10**8)()
    field = velocity.reshape(slabs, rows, lanes)
    groups = -(-slabs * rows // lanes)
    send = shape(4 * max(slabs, groups), lanes)
    *sent, metrics, x_own, y_own = call(
        send_kernel,
        [send] * len(ROUNDS)
        + [shape(TILE, lanes), shape(8, TILE, lanes), shape(12, TILE, lanes)],
        "sends",
        10**6,
    )(field, stretch, metric, tables[1])
    moved = [move(value, ways) for value, ways in zip(sent, ROUNDS)]
    bulk = call(
        bulk_kernel,
        [block, shape(lanes, groups * lanes), shape(lanes, lanes)] + [shape(8, TILE, lanes)] * 2,
        "bulk",
        10**8,
    )(field, metrics, x_own, y_own, *tables)
    (out,) = call(
        final_kernel,
        [block],
        "final",
        10**7,
    )(field, *bulk, x_own, y_own, *moved)
    return out.reshape(planes, comps, rows, lanes)


def solution(mesh):
    return jax.shard_map(
        shards,
        mesh=mesh,
        in_specs=(P(None, None, "gx", "gy"), P(), P()),
        out_specs=P(None, None, "gx", "gy"),
        check_vma=False,
    )
```

```python
import jax
import jax.numpy as jnp
import numpy as np
from jax import lax
from jax.experimental import pallas as pl
from jax.experimental.pallas import tpu as pltpu
from jax.sharding import PartitionSpec as P

VISCOSITY = 0.5
COEFS = (1.0 / 3.0, 2.0 / 11.0)
WALL_COEFS = (1.0 / 4.0, 1.0 / 10.0)
HIGHEST = lax.Precision.HIGHEST
TILE = 8
WAYS = "eo12"
ROUNDS = (
    "2oeo22eooe22oeo2",
    "o211oo2e11ooe22o",
    "1eoee1o2eo1e2oe1",
    "e1221e1122e1111e",
)


def decay(coef):
    root = (-1.0 + np.sqrt(1.0 - 4.0 * coef * coef)) / (2.0 * coef)
    return float(root), float(1.0 / (1.0 + 2.0 * coef * root))


ROOTS = tuple(decay(coef)[0] for coef in COEFS)


def inner_weights(system):
    root, gain = decay(COEFS[system])
    return (gain, gain / root, gain * root), (gain, gain * root, gain * root)


def wall_weights(system):
    root, gain = decay(COEFS[system])
    size = 96
    band = np.full(size, COEFS[system])
    band[0], band[1] = 0.0, WALL_COEFS[system]
    matrix = np.eye(size) + np.diag(band[:-1], 1) + np.diag(band[1:], -1)
    inverse = np.linalg.solve(matrix, np.eye(size)[:, :3])
    spread = (inverse[:2, 2] - gain * root ** np.abs(np.arange(2) - 2.0)) / root**2
    columns = np.stack([inverse[:2, 0], inverse[:2, 1], spread], axis=1)
    return tuple(map(float, columns[1] / root)), tuple(map(float, columns[0]))


def iota(shape, axis):
    return lax.broadcasted_iota(jnp.int32, shape, axis)


def powers(root, exponent):
    size = jnp.exp(exponent.astype(jnp.float32) * float(np.log(-root)))
    return jnp.where(lax.rem(exponent, 2) == 0, size, -size)


def stencils(minus_two, minus_one, centre, plus_one, plus_two):
    first = 7.0 / 9.0 * (plus_one - minus_one) + 1.0 / 36.0 * (plus_two - minus_two)
    second = 12.0 / 11.0 * (plus_one - 2.0 * centre + minus_one) + 3.0 / 44.0 * (
        plus_two - 2.0 * centre + minus_two
    )
    return first, second


def right_sides(lines):
    turn = lambda steps: pltpu.roll(lines, steps % lines.shape[0], 0)
    at = iota(lines.shape, 0)
    inner = (at >= 2) & (at < lines.shape[0] - 2)
    parts = stencils(turn(2), turn(1), lines, turn(-1), turn(-2))
    return [jnp.where(inner, part, 0.0) for part in parts]


def ramps(lanes):
    at = iota((TILE, lanes), 0)
    return [(powers(root, at), powers(root, TILE - 1 - at)) for root in ROOTS]


def difference_sums(lines, ramp):
    rows, lanes = lines.shape
    steps = pltpu.roll(lines, rows - 1, 0) - lines
    tiles = [steps[k : k + TILE] for k in range(0, rows, TILE)]
    tiles[-1] = jnp.where(iota((TILE, lanes), 0) == TILE - 1, 0.0, tiles[-1])
    sums = []
    for root, (up, down) in zip(ROOTS, ramp):
        step = float(root**TILE)
        reach = sum(16.0 * abs(step) ** k > np.finfo(np.float32).tiny for k in range(len(tiles)))
        near_low, near_high = tiles[:reach], tiles[len(tiles) - reach :]
        low, high = near_low[-1], near_high[0]
        for tile in near_low[-2::-1]:
            low = low * step + tile
        for tile in near_high[1:]:
            high = high * step + tile
        sums.append(jnp.sum(low * up, axis=0, keepdims=True))
        sums.append(jnp.sum(high * down, axis=0, keepdims=True))
    return sums


def right_side_sums(layers, sums, rows):
    (one, two), size = ROOTS, rows
    steps = [[line[k + 1] - line[k] for k in range(3)] for line in layers]
    bends = [[line[k + 1] - line[k] for k in range(2)] for line in steps]
    near, far = 7.0 / 9.0 + 1.0 / 36.0, 1.0 / 36.0
    mid, side = 12.0 / 11.0 + 6.0 / 44.0, 3.0 / 44.0
    result = []
    for end in range(2):
        d0, d1, d2 = steps[end]
        z0, z1, z2 = [-step for step in steps[1 - end]]
        e1, e2 = bends[end]
        y1, y2 = bends[1 - end]
        total = sums[0] if end == 0 else sums[1] * float(-1.0 / one)
        last0, last1, last2 = [z * float(one ** (size - 2 - k)) for k, z in enumerate((z0, z1, z2))]
        first = (
            near * (total - d0 - one * d1 - last0)
            + (near * one) * (total - d0 - last0 - last1)
            + (far / one) * (total - d0 - one * d1 - one * one * d2)
            + (far * one * one) * (total - last0 - last1 - last2)
        )
        total = sums[2] if end == 0 else sums[3] * float(-1.0 / two)
        total = (1.0 - two) * total - d0 + z0 * float(two ** (size - 1))
        last1, last2 = y1 * float(two ** (size - 2)), y2 * float(two ** (size - 3))
        second = (
            mid * (total - two * e1 - last1)
            + (side / two) * (total - two * e1 - two * two * e2)
            + (side * two) * (total - last1 - last2)
        )
        result.append((first if end == 0 else -first, second))
    return result


def sent_rows(layers, sums, sign):
    b1, b2, b3, b4 = layers
    d2, d3, d4 = b2 - b1, b3 - b1, b4 - b1
    one, two = ROOTS
    first = 7.0 / 9.0 * (d2 + one * d3) + 1.0 / 36.0 * (d3 + one * d4)
    second = 12.0 / 11.0 * (d2 + two * (d3 - 2.0 * d2)) + 3.0 / 44.0 * (d3 + two * (d4 - 2.0 * d2))
    return [b1, b2, sums[0] - sign * first, sums[1] + second]


def turned(field):
    slabs, rows, lanes = field.shape
    fill = -(slabs * rows) % lanes
    lines = field.reshape(slabs * rows, lanes)
    if fill:
        lines = jnp.concatenate([lines, jnp.zeros((fill, lanes), jnp.float32)], axis=0)
    return jnp.transpose(lines)


def kind_of(x, y):
    return 8 * (x % 2) + 4 * (x // 2 % 2) + 2 * (y % 2) + y // 2 % 2


def beyond(way, kind):
    return kind ^ {"e": 8, "o": 12, "1": 2, "2": 3}[way]


def arrival_rounds(way):
    return [
        next(k for k, ways in enumerate(ROUNDS) if ways[beyond(way, kind)] == way)
        for kind in range(16)
    ]


def by_kind(numbers, options):
    packed = np.int64(sum(number << 2 * kind for kind, number in enumerate(numbers)))
    kind = kind_of(lax.axis_index("gx"), lax.axis_index("gy"))
    number = lax.shift_right_logical(jnp.int32(packed.astype(np.int32)), 2 * kind) & 3
    first, *others = sorted(set(numbers))
    chosen = options[first]
    for other in others:
        chosen = jnp.where(number == other, options[other], chosen)
    return chosen


def ends_of(groups, ramp):
    rows = groups[0].shape[0]
    stack = lambda values: jnp.concatenate(values, axis=0)
    layers = [
        [stack([group[at : at + 1] for group in groups]) for at in range(4)],
        [stack([group[rows - 1 - at : rows - at] for group in groups]) for at in range(4)],
    ]
    sums = [stack(values) for values in zip(*[difference_sums(group, ramp) for group in groups])]
    return layers, right_side_sums(layers, sums, rows)


def sends(layers, sums, even):
    low = sent_rows(layers[0], sums[0], -1.0)
    high = sent_rows(layers[1], sums[1], 1.0)
    return select(even, high, low), select(even, low, high)


def send_kernel(field, stretch, metric, _, *refs):
    *outs, metrics, x_own, y_own = refs
    metrics[...] = metric_rows(stretch, metric)
    slabs, _, lanes = field.shape
    x_even = lax.rem(lax.axis_index("gx"), 2) == 0
    y_even = lax.rem(lax.axis_index("gy"), 2) == 0
    groups = [field[s] for s in range(slabs)]
    ramp = ramps(lanes)
    layers, sums = ends_of(groups, ramp)
    sent = dict(zip("eo", sends(layers, sums, x_even)))
    for k, layer in enumerate(layers[0] + layers[1]):
        x_own[k, :slabs] = layer
    lines = turned(field[...])
    layers, sums = ends_of(
        [lines[:, k : k + lanes] for k in range(0, lines.shape[1], lanes)], ramp
    )
    sent.update(zip("12", sends(layers, sums, y_even)))
    for k, values in enumerate([*layers[0], *sums[0], *layers[1], *sums[1]]):
        y_own[k, : values.shape[0]] = values
    count = outs[0].shape[0] // 4
    packed = []
    for way in WAYS:
        fill = jnp.zeros((count - sent[way][0].shape[0], lanes), jnp.float32)
        parts = [part for value in sent[way] for part in (value, fill) if part.shape[0]]
        packed.append(jnp.concatenate(parts, axis=0))
    for out, ways in zip(outs, ROUNDS):
        out[...] = by_kind([WAYS.index(way) for way in ways], packed)


def inverse_matrix(system, size):
    root, gain = decay(COEFS[system])
    return gain * powers(root, jnp.abs(iota((size, size), 0) - iota((size, size), 1)))


def solve(matrix, right_side):
    return jnp.dot(matrix, right_side, precision=HIGHEST, preferred_element_type=jnp.float32)


def table_kernel(y_out, x_out):
    for system in range(2):
        y_out[system] = inverse_matrix(system, y_out.shape[1])
        x_out[system] = inverse_matrix(system, x_out.shape[1])


def metric_rows(stretch, metric):
    position = pl.ds(lax.axis_index("gy"), 1)
    inv = 1.0 / stretch[position, :]
    curve = VISCOSITY * metric[position, :] * inv * inv * inv
    fill = jnp.zeros((TILE - 3, inv.shape[1]), jnp.float32)
    return jnp.concatenate([inv, curve, VISCOSITY * inv * inv, fill], axis=0)


def bulk_kernel(
    field, metrics, x_own, y_own, y_matrix, x_matrix,
    out, slope_turned, bend_turned, x_shares, y_shares,
):
    slabs, rows, lanes = field.shape
    y_at, y_count = lax.axis_index("gy"), lax.axis_size("gy")
    own = [x_own[k] for k in range(8)]
    shares = own_numbers(own[:4], 1.0) + own_numbers(own[4:], -1.0)
    for k, share in enumerate(shares):
        x_shares[k] = share
    own = [y_own[k] for k in range(12)]
    shares = own_numbers(own[:4], 1.0, y_at == 0, own[4:6])
    shares += own_numbers(own[6:10], -1.0, y_at == y_count - 1, own[10:])
    for k, share in enumerate(shares):
        y_shares[k] = share
    inv, curve, bend = metrics[0:1, :], metrics[1:2, :], metrics[2:3, :]
    bend = jnp.transpose(jnp.broadcast_to(bend, (lanes, lanes)))
    bend_turned[...] = bend
    slope = [-(field[plane * 3 + 1] * inv + curve) for plane in range(slabs // 3)]
    slope = turned(jnp.stack([part for part in slope for _ in range(3)], axis=0))
    slope_turned[...] = slope
    first, second = right_sides(turned(field[...]))
    y_term = slope * solve(y_matrix[0], first) + bend[:, :1] * solve(y_matrix[1], second)
    y_term = jnp.transpose(y_term)
    for s in range(slabs):
        first, second = right_sides(field[s])
        x_term = VISCOSITY * solve(x_matrix[1], second) - field[s // 3 * 3] * solve(x_matrix[0], first)
        out[s] = x_term + y_term[s * rows : (s + 1) * rows]


def weigh(weights, values):
    return weights[0] * values[0] + weights[1] * values[1] + weights[2] * values[2]


def own_numbers(own, sign, wall=None, sums=None):
    a2, a3, a4 = [layer - own[0] for layer in own[1:]]
    first = (
        sign * (7.0 / 9.0 * a2 + 1.0 / 36.0 * a3),
        sign * (7.0 / 9.0 * a3 + 1.0 / 36.0 * a4),
        sign * (1.0 / 36.0 * a2),
    )
    second = (
        12.0 / 11.0 * a2 + 3.0 / 44.0 * a3,
        12.0 / 11.0 * (a3 - 2.0 * a2) + 3.0 / 44.0 * (a4 - 2.0 * a2),
        3.0 / 44.0 * a2,
    )
    numbers = []
    for system, rows in enumerate((first, second)):
        numbers += [weigh(weights, rows) for weights in inner_weights(system)]
    if wall is None:
        return numbers
    first = (sign * (2.0 * a2 - 0.5 * a3), sign * 0.75 * a3, sums[0])
    second = (4.0 * a3 - 5.0 * a2 - a4, 1.2 * (a3 - 2.0 * a2), sums[1])
    at_wall = []
    for system, rows in enumerate((first, second)):
        at_wall += [weigh(weights, rows) for weights in wall_weights(system)]
    return [jnp.where(wall, there, here) for there, here in zip(at_wall, numbers)]


def edge_numbers(shares, nearest, received, sign, wall=None):
    b1, b2 = received[0] - nearest, received[1] - nearest
    numbers = []
    for system, root in enumerate(ROOTS):
        pair = []
        for share, (w0, w1, w2) in zip(shares[2 * system :], inner_weights(system)):
            if system == 0:
                near = -sign * (7.0 / 9.0 * (w0 + w2) + 1.0 / 36.0 * (w1 + w2 * (1.0 + root)))
                next_one = -sign * (1.0 / 36.0 * w0)
            else:
                near = 12.0 / 11.0 * (w0 - w2) + 3.0 / 44.0 * (w1 - w2 * (1.0 + root))
                next_one = 3.0 / 44.0 * w0
            part = near * b1 + next_one * b2 + w2 * received[2 + system]
            pair.append(share + (part if wall is None else jnp.where(wall, 0.0, part)))
        numbers.append(pair)
    return numbers


def edge_tiles(numbers, line, side, ramp):
    tiles = []
    for (spread, first), powers_of in zip(numbers, ramp):
        far = powers_of[side] * spread[line : line + 1]
        at_edge = iota(far.shape, 0) == (TILE - 1 if side else 0)
        tiles.append((jnp.where(at_edge, first[line : line + 1], far), far))
    return tiles


def received(way, moved, groups):
    packed = by_kind(arrival_rounds(way), [part[...] for part in moved])
    count = packed.shape[0] // 4
    return [packed[k * count : k * count + groups] for k in range(4)]


def select(flag, one, two):
    return [jnp.where(flag, there, here) for there, here in zip(one, two)]


def edge_update(low, high, root, tile, tiles):
    parts = []
    for (near, far), steps in ((low, tile), (high, tiles - 1 - tile)):
        scale = float(root ** (TILE * steps))
        if abs(scale) > np.finfo(np.float32).tiny:
            parts.append(far * scale if steps else near)
    return sum(parts[1:], parts[0]) if parts else None


def final_kernel(
    field, bulk, slope, bend, x_shares, y_shares, x_own, y_own, *refs
):
    *moved, out = refs
    slabs, rows, lanes = field.shape
    y_at, y_count = lax.axis_index("gy"), lax.axis_size("gy")
    x_even = lax.rem(lax.axis_index("gx"), 2) == 0
    y_even = lax.rem(y_at, 2) == 0
    groups = slope.shape[1] // lanes
    shares = [x_shares[k, :slabs] for k in range(8)]
    even, odd = [received(way, moved, slabs) for way in "eo"]
    x_low = edge_numbers(shares[:4], x_own[0, :slabs], select(x_even, odd, even), 1.0)
    x_high = edge_numbers(shares[4:], x_own[4, :slabs], select(x_even, even, odd), -1.0)
    for _, second in (x_low, x_high):
        second[:] = [VISCOSITY * number for number in second]
    shares = [y_shares[k, :groups] for k in range(8)]
    even, odd = [received(way, moved, groups) for way in "12"]
    from_low, from_high = select(y_even, odd, even), select(y_even, even, odd)
    low = edge_numbers(shares[:4], y_own[0, :groups], from_low, 1.0, y_at == 0)
    high = edge_numbers(shares[4:], y_own[6, :groups], from_high, -1.0, y_at == y_count - 1)
    tiles, ramp = lanes // TILE, ramps(lanes)
    y_term = []
    for group in range(groups):
        at_low, at_high = edge_tiles(low, group, 0, ramp), edge_tiles(high, group, 1, ramp)
        part = slice(group * lanes, (group + 1) * lanes)
        column = []
        for tile in range(tiles):
            place = slice(tile * TILE, (tile + 1) * TILE)
            one, two = [edge_update(at_low[k], at_high[k], ROOTS[k], tile, tiles) for k in range(2)]
            term = slope[place, part] * one
            column.append(term if two is None else term + bend[place, :] * two)
        y_term.append(jnp.transpose(jnp.concatenate(column, axis=0)))
    y_term = jnp.concatenate(y_term, axis=0)
    tiles = rows // TILE
    for s in range(slabs):
        at_low, at_high = edge_tiles(x_low, s, 0, ramp), edge_tiles(x_high, s, 1, ramp)
        for tile in range(tiles):
            place = slice(tile * TILE, (tile + 1) * TILE)
            one, two = [edge_update(at_low[k], at_high[k], ROOTS[k], tile, tiles) for k in range(2)]
            turned = y_term[s * rows + tile * TILE : s * rows + (tile + 1) * TILE]
            x_term = two - field[s // 3 * 3, place] * one
            out[s, place] = bulk[s, place] + x_term + turned


def partner(way, x, y, x_count, y_count):
    if way == "2" and y in (0, y_count - 1):
        way = "e"
    if way in "eo":
        step = 1 if (x % 2 == 0) == (way == "e") else -1
        return (x + step) % x_count, y
    return x, y + (1 if (y % 2 == 0) == (way == "1") else -1)


def exchange_pairs(ways, x_count, y_count):
    at = lambda x, y: x * y_count + y
    return [
        (at(x, y), at(*partner(ways[kind_of(x, y)], x, y, x_count, y_count)))
        for x in range(x_count)
        for y in range(y_count)
    ]


def call(kernel, outs, name, flops, out_space=pltpu.VMEM, scratch=()):
    return lambda *args: pl.pallas_call(
        kernel,
        out_shape=outs,
        in_specs=[pl.BlockSpec(memory_space=pltpu.VMEM)] * len(args),
        out_specs=[pl.BlockSpec(memory_space=out_space)] * len(outs),
        scratch_shapes=scratch,
        cost_estimate=pl.CostEstimate(flops=flops, bytes_accessed=0, transcendentals=0),
        compiler_params=pltpu.CompilerParams(vmem_limit_bytes=8 * 2**20),
        name=name,
    )(*args)


def shards(velocity, stretch, second_metric):
    planes, comps, rows, lanes = velocity.shape
    slabs = planes * comps
    x_count, y_count = lax.axis_size("gx"), lax.axis_size("gy")
    stretch = stretch.reshape(y_count, lanes)
    metric = second_metric.reshape(y_count, lanes)
    shape = lambda *dims: jax.ShapeDtypeStruct(dims, jnp.float32)
    block = shape(slabs, rows, lanes)
    move = lambda value, ways: lax.ppermute(
        value, ("gx", "gy"), exchange_pairs(ways, x_count, y_count)
    )

    tables = call(table_kernel, [shape(2, lanes, lanes), shape(2, rows, rows)], "tables", 10**8)()
    field = velocity.reshape(slabs, rows, lanes)
    groups = -(-slabs * rows // lanes)
    send = shape(4 * max(slabs, groups), lanes)
    *sent, metrics, x_own, y_own = call(
        send_kernel,
        [send] * len(ROUNDS)
        + [shape(TILE, lanes), shape(8, TILE, lanes), shape(12, TILE, lanes)],
        "sends",
        10**6,
    )(field, stretch, metric, tables[1])
    moved = [move(value, ways) for value, ways in zip(sent, ROUNDS)]
    bulk = call(
        bulk_kernel,
        [block, shape(lanes, groups * lanes), shape(lanes, lanes)] + [shape(8, TILE, lanes)] * 2,
        "bulk",
        10**8,
    )(field, metrics, x_own, y_own, *tables)
    (out,) = call(
        final_kernel,
        [block],
        "final",
        10**7,
    )(field, *bulk, x_own, y_own, *moved)
    return out.reshape(planes, comps, rows, lanes)


def solution(mesh):
    return jax.shard_map(
        shards,
        mesh=mesh,
        in_specs=(P(None, None, "gx", "gy"), P(), P()),
        out_specs=P(None, None, "gx", "gy"),
        check_vma=False,
    )
```

```python
import jax
import jax.numpy as jnp
import numpy as np
from jax import lax
from jax.experimental import pallas as pl
from jax.experimental.pallas import tpu as pltpu
from jax.sharding import PartitionSpec as P

VISCOSITY = 0.5
COEFS = (1.0 / 3.0, 2.0 / 11.0)
WALL_COEFS = (1.0 / 4.0, 1.0 / 10.0)
HIGHEST = lax.Precision.HIGHEST
TILE = 8
WAYS = "eo12"
ROUNDS = (
    "2oeo22eooe22oeo2",
    "o211oo2e11ooe22o",
    "1eoee1o2eo1e2oe1",
    "e1221e1122e1111e",
)


def decay(coef):
    root = (-1.0 + np.sqrt(1.0 - 4.0 * coef * coef)) / (2.0 * coef)
    return float(root), float(1.0 / (1.0 + 2.0 * coef * root))


ROOTS = tuple(decay(coef)[0] for coef in COEFS)


def inner_weights(system):
    root, gain = decay(COEFS[system])
    return (gain, gain / root, gain * root), (gain, gain * root, gain * root)


def wall_weights(system):
    root, gain = decay(COEFS[system])
    size = 96
    band = np.full(size, COEFS[system])
    band[0], band[1] = 0.0, WALL_COEFS[system]
    matrix = np.eye(size) + np.diag(band[:-1], 1) + np.diag(band[1:], -1)
    inverse = np.linalg.solve(matrix, np.eye(size)[:, :3])
    spread = (inverse[:2, 2] - gain * root ** np.abs(np.arange(2) - 2.0)) / root**2
    columns = np.stack([inverse[:2, 0], inverse[:2, 1], spread], axis=1)
    return tuple(map(float, columns[1] / root)), tuple(map(float, columns[0]))


def iota(shape, axis):
    return lax.broadcasted_iota(jnp.int32, shape, axis)


def powers(root, exponent):
    size = jnp.exp(exponent.astype(jnp.float32) * float(np.log(-root)))
    return jnp.where(lax.rem(exponent, 2) == 0, size, -size)


def stencils(minus_two, minus_one, centre, plus_one, plus_two):
    first = 7.0 / 9.0 * (plus_one - minus_one) + 1.0 / 36.0 * (plus_two - minus_two)
    second = 12.0 / 11.0 * (plus_one - 2.0 * centre + minus_one) + 3.0 / 44.0 * (
        plus_two - 2.0 * centre + minus_two
    )
    return first, second


def right_sides(lines):
    turn = lambda steps: pltpu.roll(lines, steps % lines.shape[0], 0)
    at = iota(lines.shape, 0)
    inner = (at >= 2) & (at < lines.shape[0] - 2)
    parts = stencils(turn(2), turn(1), lines, turn(-1), turn(-2))
    return [jnp.where(inner, part, 0.0) for part in parts]


def ramps(lanes):
    at = iota((TILE, lanes), 0)
    return [(powers(root, at), powers(root, TILE - 1 - at)) for root in ROOTS]


def difference_sums(lines, ramp):
    rows, lanes = lines.shape
    steps = pltpu.roll(lines, rows - 1, 0) - lines
    tiles = [steps[k : k + TILE] for k in range(0, rows, TILE)]
    tiles[-1] = jnp.where(iota((TILE, lanes), 0) == TILE - 1, 0.0, tiles[-1])
    sums = []
    for root, (up, down) in zip(ROOTS, ramp):
        step = float(root**TILE)
        reach = sum(16.0 * abs(step) ** k > np.finfo(np.float32).tiny for k in range(len(tiles)))
        near_low, near_high = tiles[:reach], tiles[len(tiles) - reach :]
        low, high = near_low[-1], near_high[0]
        for tile in near_low[-2::-1]:
            low = low * step + tile
        for tile in near_high[1:]:
            high = high * step + tile
        sums.append(jnp.sum(low * up, axis=0, keepdims=True))
        sums.append(jnp.sum(high * down, axis=0, keepdims=True))
    return sums


def right_side_sums(layers, sums, rows):
    (one, two), size = ROOTS, rows
    steps = [[line[k + 1] - line[k] for k in range(3)] for line in layers]
    bends = [[line[k + 1] - line[k] for k in range(2)] for line in steps]
    near, far = 7.0 / 9.0 + 1.0 / 36.0, 1.0 / 36.0
    mid, side = 12.0 / 11.0 + 6.0 / 44.0, 3.0 / 44.0
    result = []
    for end in range(2):
        d0, d1, d2 = steps[end]
        z0, z1, z2 = [-step for step in steps[1 - end]]
        e1, e2 = bends[end]
        y1, y2 = bends[1 - end]
        total = sums[0] if end == 0 else sums[1] * float(-1.0 / one)
        last0, last1, last2 = [z * float(one ** (size - 2 - k)) for k, z in enumerate((z0, z1, z2))]
        first = (
            near * (total - d0 - one * d1 - last0)
            + (near * one) * (total - d0 - last0 - last1)
            + (far / one) * (total - d0 - one * d1 - one * one * d2)
            + (far * one * one) * (total - last0 - last1 - last2)
        )
        total = sums[2] if end == 0 else sums[3] * float(-1.0 / two)
        total = (1.0 - two) * total - d0 + z0 * float(two ** (size - 1))
        last1, last2 = y1 * float(two ** (size - 2)), y2 * float(two ** (size - 3))
        second = (
            mid * (total - two * e1 - last1)
            + (side / two) * (total - two * e1 - two * two * e2)
            + (side * two) * (total - last1 - last2)
        )
        result.append((first if end == 0 else -first, second))
    return result


def sent_rows(layers, sums, sign):
    b1, b2, b3, b4 = layers
    d2, d3, d4 = b2 - b1, b3 - b1, b4 - b1
    one, two = ROOTS
    first = 7.0 / 9.0 * (d2 + one * d3) + 1.0 / 36.0 * (d3 + one * d4)
    second = 12.0 / 11.0 * (d2 + two * (d3 - 2.0 * d2)) + 3.0 / 44.0 * (d3 + two * (d4 - 2.0 * d2))
    return [b1, b2, sums[0] - sign * first, sums[1] + second]


def turned(field):
    slabs, rows, lanes = field.shape
    fill = -(slabs * rows) % lanes
    lines = field.reshape(slabs * rows, lanes)
    if fill:
        lines = jnp.concatenate([lines, jnp.zeros((fill, lanes), jnp.float32)], axis=0)
    return jnp.transpose(lines)


def kind_of(x, y):
    return 8 * (x % 2) + 4 * (x // 2 % 2) + 2 * (y % 2) + y // 2 % 2


def beyond(way, kind):
    return kind ^ {"e": 8, "o": 12, "1": 2, "2": 3}[way]


def arrival_rounds(way):
    return [
        next(k for k, ways in enumerate(ROUNDS) if ways[beyond(way, kind)] == way)
        for kind in range(16)
    ]


def by_kind(numbers, options):
    packed = np.int64(sum(number << 2 * kind for kind, number in enumerate(numbers)))
    kind = kind_of(lax.axis_index("gx"), lax.axis_index("gy"))
    number = lax.shift_right_logical(jnp.int32(packed.astype(np.int32)), 2 * kind) & 3
    first, *others = sorted(set(numbers))
    chosen = options[first]
    for other in others:
        chosen = jnp.where(number == other, options[other], chosen)
    return chosen


def ends_of(groups, ramp):
    rows = groups[0].shape[0]
    stack = lambda values: jnp.concatenate(values, axis=0)
    layers = [
        [stack([group[at : at + 1] for group in groups]) for at in range(4)],
        [stack([group[rows - 1 - at : rows - at] for group in groups]) for at in range(4)],
    ]
    sums = [stack(values) for values in zip(*[difference_sums(group, ramp) for group in groups])]
    return layers, right_side_sums(layers, sums, rows)


def sends(layers, sums, even):
    low = sent_rows(layers[0], sums[0], -1.0)
    high = sent_rows(layers[1], sums[1], 1.0)
    return select(even, high, low), select(even, low, high)


def send_kernel(field, stretch, metric, ramp_in, *refs):
    *outs, metrics, x_own, y_own = refs
    metrics[...] = metric_rows(stretch, metric)
    slabs, _, lanes = field.shape
    x_even = lax.rem(lax.axis_index("gx"), 2) == 0
    y_even = lax.rem(lax.axis_index("gy"), 2) == 0
    groups = [field[s] for s in range(slabs)]
    ramp = [(ramp_in[0], ramp_in[1]), (ramp_in[2], ramp_in[3])]
    layers, sums = ends_of(groups, ramp)
    sent = dict(zip("eo", sends(layers, sums, x_even)))
    for k, layer in enumerate(layers[0] + layers[1]):
        x_own[k, :slabs] = layer
    lines = turned(field[...])
    layers, sums = ends_of(
        [lines[:, k : k + lanes] for k in range(0, lines.shape[1], lanes)], ramp
    )
    sent.update(zip("12", sends(layers, sums, y_even)))
    for k, values in enumerate([*layers[0], *sums[0], *layers[1], *sums[1]]):
        y_own[k, : values.shape[0]] = values
    count = outs[0].shape[0] // 4
    packed = []
    for way in WAYS:
        fill = jnp.zeros((count - sent[way][0].shape[0], lanes), jnp.float32)
        parts = [part for value in sent[way] for part in (value, fill) if part.shape[0]]
        packed.append(jnp.concatenate(parts, axis=0))
    for out, ways in zip(outs, ROUNDS):
        out[...] = by_kind([WAYS.index(way) for way in ways], packed)


def inverse_matrix(system, size):
    root, gain = decay(COEFS[system])
    return gain * powers(root, jnp.abs(iota((size, size), 0) - iota((size, size), 1)))


def solve(matrix, right_side):
    return jnp.dot(matrix, right_side, precision=HIGHEST, preferred_element_type=jnp.float32)


def table_kernel(y_out, x_out, ramp_out):
    for k, ramp in enumerate(ramps(y_out.shape[1])):
        ramp_out[2 * k], ramp_out[2 * k + 1] = ramp
    for system in range(2):
        y_out[system] = inverse_matrix(system, y_out.shape[1])
        x_out[system] = inverse_matrix(system, x_out.shape[1])


def metric_rows(stretch, metric):
    position = pl.ds(lax.axis_index("gy"), 1)
    inv = 1.0 / stretch[position, :]
    curve = VISCOSITY * metric[position, :] * inv * inv * inv
    fill = jnp.zeros((TILE - 3, inv.shape[1]), jnp.float32)
    return jnp.concatenate([inv, curve, VISCOSITY * inv * inv, fill], axis=0)


def bulk_kernel(
    field, metrics, x_own, y_own, y_matrix, x_matrix,
    out, slope_turned, bend_turned, x_shares, y_shares,
):
    slabs, rows, lanes = field.shape
    y_at, y_count = lax.axis_index("gy"), lax.axis_size("gy")
    own = [x_own[k] for k in range(8)]
    shares = own_numbers(own[:4], 1.0) + own_numbers(own[4:], -1.0)
    for k, share in enumerate(shares):
        x_shares[k] = share
    own = [y_own[k] for k in range(12)]
    shares = own_numbers(own[:4], 1.0, y_at == 0, own[4:6])
    shares += own_numbers(own[6:10], -1.0, y_at == y_count - 1, own[10:])
    for k, share in enumerate(shares):
        y_shares[k] = share
    inv, curve, bend = metrics[0:1, :], metrics[1:2, :], metrics[2:3, :]
    bend = jnp.transpose(jnp.broadcast_to(bend, (lanes, lanes)))
    bend_turned[...] = bend
    slope = [-(field[plane * 3 + 1] * inv + curve) for plane in range(slabs // 3)]
    slope = turned(jnp.stack([part for part in slope for _ in range(3)], axis=0))
    slope_turned[...] = slope
    first, second = right_sides(turned(field[...]))
    y_term = slope * solve(y_matrix[0], first) + bend[:, :1] * solve(y_matrix[1], second)
    y_term = jnp.transpose(y_term)
    for s in range(slabs):
        first, second = right_sides(field[s])
        x_term = VISCOSITY * solve(x_matrix[1], second) - field[s // 3 * 3] * solve(x_matrix[0], first)
        out[s] = x_term + y_term[s * rows : (s + 1) * rows]


def weigh(weights, values):
    return weights[0] * values[0] + weights[1] * values[1] + weights[2] * values[2]


def own_numbers(own, sign, wall=None, sums=None):
    a2, a3, a4 = [layer - own[0] for layer in own[1:]]
    first = (
        sign * (7.0 / 9.0 * a2 + 1.0 / 36.0 * a3),
        sign * (7.0 / 9.0 * a3 + 1.0 / 36.0 * a4),
        sign * (1.0 / 36.0 * a2),
    )
    second = (
        12.0 / 11.0 * a2 + 3.0 / 44.0 * a3,
        12.0 / 11.0 * (a3 - 2.0 * a2) + 3.0 / 44.0 * (a4 - 2.0 * a2),
        3.0 / 44.0 * a2,
    )
    numbers = []
    for system, rows in enumerate((first, second)):
        numbers += [weigh(weights, rows) for weights in inner_weights(system)]
    if wall is None:
        return numbers
    first = (sign * (2.0 * a2 - 0.5 * a3), sign * 0.75 * a3, sums[0])
    second = (4.0 * a3 - 5.0 * a2 - a4, 1.2 * (a3 - 2.0 * a2), sums[1])
    at_wall = []
    for system, rows in enumerate((first, second)):
        at_wall += [weigh(weights, rows) for weights in wall_weights(system)]
    return [jnp.where(wall, there, here) for there, here in zip(at_wall, numbers)]


def edge_numbers(shares, nearest, received, sign, wall=None):
    b1, b2 = received[0] - nearest, received[1] - nearest
    numbers = []
    for system, root in enumerate(ROOTS):
        pair = []
        for share, (w0, w1, w2) in zip(shares[2 * system :], inner_weights(system)):
            if system == 0:
                near = -sign * (7.0 / 9.0 * (w0 + w2) + 1.0 / 36.0 * (w1 + w2 * (1.0 + root)))
                next_one = -sign * (1.0 / 36.0 * w0)
            else:
                near = 12.0 / 11.0 * (w0 - w2) + 3.0 / 44.0 * (w1 - w2 * (1.0 + root))
                next_one = 3.0 / 44.0 * w0
            part = near * b1 + next_one * b2 + w2 * received[2 + system]
            pair.append(share + (part if wall is None else jnp.where(wall, 0.0, part)))
        numbers.append(pair)
    return numbers


def edge_tiles(numbers, line, side, ramp):
    tiles = []
    for (spread, first), powers_of in zip(numbers, ramp):
        far = powers_of[side] * spread[line : line + 1]
        at_edge = iota(far.shape, 0) == (TILE - 1 if side else 0)
        tiles.append((jnp.where(at_edge, first[line : line + 1], far), far))
    return tiles


def received(way, moved, groups):
    packed = by_kind(arrival_rounds(way), [part[...] for part in moved])
    count = packed.shape[0] // 4
    return [packed[k * count : k * count + groups] for k in range(4)]


def select(flag, one, two):
    return [jnp.where(flag, there, here) for there, here in zip(one, two)]


def edge_update(low, high, root, tile, tiles):
    parts = []
    for (near, far), steps in ((low, tile), (high, tiles - 1 - tile)):
        scale = float(root ** (TILE * steps))
        if abs(scale) > np.finfo(np.float32).tiny:
            parts.append(far * scale if steps else near)
    return sum(parts[1:], parts[0]) if parts else None


def final_kernel(
    field, bulk, slope, bend, x_shares, y_shares, x_own, y_own, ramp_in, *refs
):
    *moved, out = refs
    slabs, rows, lanes = field.shape
    y_at, y_count = lax.axis_index("gy"), lax.axis_size("gy")
    x_even = lax.rem(lax.axis_index("gx"), 2) == 0
    y_even = lax.rem(y_at, 2) == 0
    groups = slope.shape[1] // lanes
    shares = [y_shares[k, :groups] for k in range(8)]
    even, odd = [received(way, moved, groups) for way in "12"]
    from_low, from_high = select(y_even, odd, even), select(y_even, even, odd)
    low = edge_numbers(shares[:4], y_own[0, :groups], from_low, 1.0, y_at == 0)
    high = edge_numbers(shares[4:], y_own[6, :groups], from_high, -1.0, y_at == y_count - 1)
    tiles = lanes // TILE
    ramp = [(ramp_in[0], ramp_in[1]), (ramp_in[2], ramp_in[3])]
    y_term = []
    for group in range(groups):
        at_low, at_high = edge_tiles(low, group, 0, ramp), edge_tiles(high, group, 1, ramp)
        part = slice(group * lanes, (group + 1) * lanes)
        column = []
        for tile in range(tiles):
            place = slice(tile * TILE, (tile + 1) * TILE)
            one, two = [edge_update(at_low[k], at_high[k], ROOTS[k], tile, tiles) for k in range(2)]
            term = slope[place, part] * one
            column.append(term if two is None else term + bend[place, :] * two)
        y_term.append(jnp.transpose(jnp.concatenate(column, axis=0)))
    y_term = jnp.concatenate(y_term, axis=0)
    shares = [x_shares[k, :slabs] for k in range(8)]
    even, odd = [received(way, moved, slabs) for way in "eo"]
    low = edge_numbers(shares[:4], x_own[0, :slabs], select(x_even, odd, even), 1.0)
    high = edge_numbers(shares[4:], x_own[4, :slabs], select(x_even, even, odd), -1.0)
    for _, second in (low, high):
        second[:] = [VISCOSITY * number for number in second]
    tiles = rows // TILE
    for s in range(slabs):
        at_low, at_high = edge_tiles(low, s, 0, ramp), edge_tiles(high, s, 1, ramp)
        for tile in range(tiles):
            place = slice(tile * TILE, (tile + 1) * TILE)
            one, two = [edge_update(at_low[k], at_high[k], ROOTS[k], tile, tiles) for k in range(2)]
            turned = y_term[s * rows + tile * TILE : s * rows + (tile + 1) * TILE]
            x_term = two - field[s // 3 * 3, place] * one
            out[s, place] = bulk[s, place] + x_term + turned


def partner(way, x, y, x_count, y_count):
    if way == "2" and y in (0, y_count - 1):
        way = "e"
    if way in "eo":
        step = 1 if (x % 2 == 0) == (way == "e") else -1
        return (x + step) % x_count, y
    return x, y + (1 if (y % 2 == 0) == (way == "1") else -1)


def exchange_pairs(ways, x_count, y_count):
    at = lambda x, y: x * y_count + y
    return [
        (at(x, y), at(*partner(ways[kind_of(x, y)], x, y, x_count, y_count)))
        for x in range(x_count)
        for y in range(y_count)
    ]


def call(kernel, outs, name, flops, out_space=pltpu.VMEM, scratch=()):
    return lambda *args: pl.pallas_call(
        kernel,
        out_shape=outs,
        in_specs=[pl.BlockSpec(memory_space=pltpu.VMEM)] * len(args),
        out_specs=[pl.BlockSpec(memory_space=out_space)] * len(outs),
        scratch_shapes=scratch,
        cost_estimate=pl.CostEstimate(flops=flops, bytes_accessed=0, transcendentals=0),
        compiler_params=pltpu.CompilerParams(vmem_limit_bytes=8 * 2**20),
        name=name,
    )(*args)


def shards(velocity, stretch, second_metric):
    planes, comps, rows, lanes = velocity.shape
    slabs = planes * comps
    x_count, y_count = lax.axis_size("gx"), lax.axis_size("gy")
    stretch = stretch.reshape(y_count, lanes)
    metric = second_metric.reshape(y_count, lanes)
    shape = lambda *dims: jax.ShapeDtypeStruct(dims, jnp.float32)
    block = shape(slabs, rows, lanes)
    move = lambda value, ways: lax.ppermute(
        value, ("gx", "gy"), exchange_pairs(ways, x_count, y_count)
    )

    *tables, ramp = call(table_kernel, [shape(2, lanes, lanes), shape(2, rows, rows), shape(4, TILE, lanes)], "tables", 10**8)()
    field = velocity.reshape(slabs, rows, lanes)
    groups = -(-slabs * rows // lanes)
    send = shape(4 * max(slabs, groups), lanes)
    *sent, metrics, x_own, y_own = call(
        send_kernel,
        [send] * len(ROUNDS)
        + [shape(TILE, lanes), shape(8, TILE, lanes), shape(12, TILE, lanes)],
        "sends",
        10**6,
    )(field, stretch, metric, ramp)
    moved = [move(value, ways) for value, ways in zip(sent, ROUNDS)]
    bulk = call(
        bulk_kernel,
        [block, shape(lanes, groups * lanes), shape(lanes, lanes)] + [shape(8, TILE, lanes)] * 2,
        "bulk",
        10**8,
    )(field, metrics, x_own, y_own, *tables)
    (out,) = call(
        final_kernel,
        [block],
        "final",
        10**7,
    )(field, *bulk, x_own, y_own, ramp, *moved)
    return out.reshape(planes, comps, rows, lanes)


def solution(mesh):
    return jax.shard_map(
        shards,
        mesh=mesh,
        in_specs=(P(None, None, "gx", "gy"), P(), P()),
        out_specs=P(None, None, "gx", "gy"),
        check_vma=False,
    )
```
